32 devices in a mesh: groups: 1, tensor: 32 (over z, y, x, core).
Axes of the slice: x: 2, y: 2, z: 4, core: 2. Of those that a mesh axis runs over, the one named last changes fastest.
Arguments:
- hidden: bfloat16 [24, 8192], P('groups', 'tensor'), may hold values from -10 to 10
- w_qkv: bfloat16 [8192, 5120], P('tensor'), may hold values from -0.0625 to 0.0625
- key_cache: bfloat16 [24, 8192, 512], P('groups', 'tensor'), may hold values from -6 to 6
- value_cache: bfloat16 [24, 8192, 512], P('groups', 'tensor'), may hold values from -24 to 24
- lengths: int32 [24], P('groups'), may hold values from 1024 to 8192
- w_out: bfloat16 [4096, 8192], P(None, 'tensor'), may hold values from -0.25 to 0.25
- w_gate: bfloat16 [8192, 14336], P(None, 'tensor'), may hold values from -0.0625 to 0.0625
- w_up: bfloat16 [8192, 14336], P(None, 'tensor'), may hold values from -0.0625 to 0.0625
- w_down: bfloat16 [14336, 8192], P('tensor'), may hold values from -0.09375 to 0.09375
Outputs:
- output: bfloat16 [24, 8192], P('groups', 'tensor')
The draws below stay inside these ranges and needn't reach their ends.
All inputs are finite; a program needn't handle non-finite values.
Results may differ from the reference program's by a relative error of at most 0.009.
Values may be sent and summed in bfloat16 or wider, within the bound.
No kernel may reach another device: no remote copies, remote signals or barrier semaphores. Data moves between devices by JAX's collectives and lax.ppermute only.
A program may use at most 128 MiB of HBM per device.

```python
import jax
import jax.numpy as jnp
import numpy as np
from jax import lax

D = 8192
FF = 14336
H = 32
KVH = 4
HD = 128
CTX = 8192
ROWS = 24


def draw_hidden(key, part):
    key = jax.random.fold_in(key, 11)
    first_key, second_key, third_key = jax.random.split(key, 3)
    position = jnp.arange(D, dtype=jnp.float32) / D
    row_factor = jnp.exp(jax.random.uniform(second_key, (ROWS, 1), jnp.float32, jnp.log(0.8), jnp.log(1.25)))
    column_factor = 0.25 * jnp.exp(jnp.log(3.0) * position) * jnp.exp(jax.random.uniform(first_key, (D,), jnp.float32, 0.0, jnp.log(3.3)))
    base = jnp.clip(jax.random.normal(third_key, (ROWS, D), jnp.float32), -3.0, 3.0)
    return (base * column_factor[None, :] * row_factor).astype(jnp.bfloat16)


def draw_lengths(key, part):
    key = jax.random.fold_in(key, 7)
    first_key, second_key = jax.random.split(key)
    drawn = jax.random.randint(first_key, (ROWS,), CTX // 8, CTX + 1)
    chosen = jax.random.randint(second_key, (), 0, ROWS)
    return jnp.where(jnp.arange(ROWS) == chosen, CTX, drawn).astype(jnp.int32)


def strengthened(values, stream_key, source, target, shards_of, factor):
    owner, partner = [(jnp.arange(values.shape[dim]) // (values.shape[dim] // shards_of)).reshape([-1 if axis == dim else 1 for axis in range(values.ndim)]) for dim in (source, target)]
    chosen = jax.random.permutation(stream_key, shards_of)[partner]
    strong = (owner == chosen) | (owner == (partner + shards_of // 2) % shards_of)
    return jnp.where(strong, factor * values, values)


def levels(rng, extent, shards, least, high):
    gain, own = 1.0, jax.random.fold_in(rng, 6)
    for dim, shards_of in shards:
        heights = jnp.exp(jax.random.uniform(jax.random.fold_in(own, dim), (shards_of,), jnp.float32, least / len(shards), high / len(shards)))
        gain = gain * jnp.repeat(heights, extent[dim] // shards_of).reshape([-1 if axis == dim else 1 for axis in range(len(extent))])
    return gain


def bell_draw(stream_key, dims, deviation, reach, cuts=(), kind=jnp.bfloat16):
    gain = levels(stream_key, dims, cuts, -0.22, 0.18) if cuts else 1.0
    values = jax.random.normal(stream_key, dims, jnp.float32) * deviation * gain
    return jnp.minimum(jnp.maximum(values, -reach), reach).astype(kind)


def noise_with(key, dims, deviation, bound, cuts, heavy, held_as=jnp.bfloat16):
    values = deviation * jax.random.normal(key, dims, jnp.float32)
    if cuts:
        values = values * levels(key, dims, cuts, -0.22, 0.18)
    return jnp.clip(strengthened(values, jax.random.fold_in(key, 3), *heavy), -bound, bound).astype(held_as)


def setup_inputs(seed: int = 0, part: int = 0) -> dict:
    streams_of = jax.random.split(jax.random.key(seed), 10)
    part_keys = jax.random.split(jax.random.fold_in(streams_of[9], part), 10)
    return {
        "hidden": draw_hidden(jax.random.fold_in(jax.random.fold_in(streams_of[9], part), 71), part),
        "w_qkv": bell_draw(streams_of[1], (D, (H + 2 * KVH) * HD), D ** -0.5, 0.0625, ((0, 32),)),
        "key_cache": bell_draw(part_keys[2], (ROWS, CTX, KVH * HD), 1.0, 6.0, ((1, 32),)),
        "value_cache": bell_draw(part_keys[3], (ROWS, CTX, KVH * HD), 4.0, 24.0, ((1, 32),)),
        "lengths": draw_lengths(jax.random.fold_in(jax.random.fold_in(streams_of[9], part), 71), part),
        "w_out": bell_draw(streams_of[5], (H * HD, D), (KVH * HD) ** -0.5, 0.25, ((1, 32),)),
        "w_gate": bell_draw(streams_of[6], (D, FF), D ** -0.5, 0.0625, ((1, 32),)),
        "w_up": bell_draw(streams_of[7], (D, FF), D ** -0.5, 0.0625, ((1, 32),)),
        "w_down": noise_with(streams_of[8], (FF, D), FF ** -0.5, 0.09375, ((0, 32),), (0, 1, 32, 2.75)),
    }


EPSILON = 1e-05
ROPE_BASE = 500000.0

def paley_table():
    prime = 13
    residues = [value * value % prime for value in range(1, prime)]
    conference = np.zeros((prime + 1, prime + 1))
    conference[0, 1:] = 1.0
    conference[1:, 0] = 1.0
    for row_number in range(prime):
        for col_number in range(prime):
            offset = (col_number - row_number) % prime
            if offset != 0:
                conference[row_number + 1, col_number + 1] = 1.0 if offset in residues else -1.0
    first_block = np.array([[1.0, -1.0], [-1.0, -1.0]])
    second_block = np.array([[1.0, 1.0], [1.0, -1.0]])
    return np.kron(conference, first_block) + np.kron(np.eye(prime + 1), second_block)

def sylvester_table(order):
    result = np.ones((1, 1))
    while result.shape[0] < order:
        result = np.kron(np.array([[1.0, 1.0], [1.0, -1.0]]), result)
    return result

def rotary(values, positions):
    half_width = values.shape[-1] // 2
    frequency = ROPE_BASE ** (-2.0 * jnp.arange(half_width, dtype=jnp.float32) / values.shape[-1])
    angles = positions.astype(jnp.float32)[:, None, None] * frequency[None, None, :]
    cosine = jnp.cos(angles)
    sine = jnp.sin(angles)
    front = values[..., :half_width]
    back = values[..., half_width:]
    return jnp.concatenate([front * cosine - back * sine, back * cosine + front * sine], axis=-1)

def reference(hidden, w_qkv, key_cache, value_cache, lengths, w_out, w_gate, w_up, w_down):
    row_count = hidden.shape[0]
    query_width = H * HD
    kv_width = KVH * HD
    group_size = H // KVH
    score_scale = HD ** (-0.5)
    hidden_wide = hidden.astype(jnp.float32)
    inverse = lax.rsqrt(lax.optimization_barrier(jnp.mean(hidden_wide * hidden_wide, axis=1, keepdims=True)) + EPSILON)
    projected = jnp.dot(hidden, w_qkv, preferred_element_type=jnp.float32)
    qkv = (projected * inverse).astype(jnp.bfloat16)
    queries = rotary(qkv[:, :query_width].astype(jnp.float32).reshape(row_count, H, HD), lengths).astype(jnp.bfloat16)
    keys_new = rotary(qkv[:, query_width:query_width + kv_width].astype(jnp.float32).reshape(row_count, KVH, HD), lengths).astype(jnp.bfloat16)
    values_new = qkv[:, query_width + kv_width:].reshape(row_count, KVH, HD)
    grouped = queries.astype(jnp.float32).reshape(row_count, KVH, group_size, HD)
    positions = jnp.arange(CTX)

    def one_row(inputs):
        query, keys, values, length = inputs
        keys = keys.astype(jnp.float32).reshape(CTX, KVH, HD)
        values = values.astype(jnp.float32).reshape(CTX, KVH, HD)
        scores = jnp.einsum('kgd,ckd->kgc', query, keys, precision=lax.Precision.HIGHEST) * score_scale
        weights = jnp.where(positions[None, None, :] < length, jnp.exp(scores), jnp.float32(0.0))
        totals_row = lax.optimization_barrier(jnp.sum(weights, axis=2))
        rounded = lax.optimization_barrier(weights.astype(jnp.bfloat16)).astype(jnp.float32)
        summed_row = jnp.einsum('kgc,ckd->kgd', rounded, values, precision=lax.Precision.HIGHEST)
        return (totals_row, summed_row)
    totals, summed = lax.map(one_row, (grouped, key_cache, value_cache, lengths))
    own_scores = jnp.einsum('rkgd,rkd->rkg', grouped, keys_new.astype(jnp.float32), precision=lax.Precision.HIGHEST) * score_scale
    own_weights = jnp.exp(own_scores)
    totals = totals + own_weights
    summed = summed + own_weights[..., None] * values_new.astype(jnp.float32)[:, :, None, :]
    attention = (summed / totals[..., None]).reshape(row_count, query_width).astype(jnp.bfloat16)
    residual = (hidden_wide + jnp.dot(attention, w_out, preferred_element_type=jnp.float32)).astype(jnp.bfloat16)
    residual_wide = residual.astype(jnp.float32)
    normed = (residual_wide * lax.rsqrt(lax.optimization_barrier(jnp.mean(residual_wide * residual_wide, axis=1, keepdims=True)) + EPSILON)).astype(jnp.bfloat16)
    gate = jnp.dot(normed, w_gate, preferred_element_type=jnp.float32)
    upward = jnp.dot(normed, w_up, preferred_element_type=jnp.float32)
    activation = jax.nn.silu(gate) * upward
    paley = jnp.asarray(paley_table(), dtype=jnp.float32)
    sylvester = jnp.asarray(sylvester_table(FF // 28), dtype=jnp.float32)
    shaped = activation.reshape(row_count, FF // 28, 28)
    inner = jnp.einsum('rsa,ea->rse', shaped, paley, precision=lax.Precision.HIGHEST)
    outer = jnp.einsum('rse,ts->rte', inner, sylvester, precision=lax.Precision.HIGHEST)
    rotated = (outer.reshape(row_count, FF) * FF ** (-0.5)).astype(jnp.bfloat16)
    down = jnp.dot(rotated, w_down, preferred_element_type=jnp.float32)
    return (residual_wide + down).astype(jnp.bfloat16)
```

```python
import jax
import jax.numpy as jnp
import numpy as np
from jax import lax
from jax.sharding import PartitionSpec as P

D = 8192
FF = 14336
H = 32
KVH = 4
HD = 128


EPSILON = 1e-05
ROPE_BASE = 500000.0


def scattered_sum(pieces):
    received = lax.all_to_all(pieces, "tensor", 0, 0, tiled=True)
    return jnp.sum(received.astype(jnp.float32), axis=0)


def gathered(piece):
    copies = jnp.broadcast_to(piece[None], (lax.axis_size("tensor"), *piece.shape))
    return lax.all_to_all(copies, "tensor", 0, 0, tiled=True)


def paley_table():
    prime = 13
    residues = [value * value % prime for value in range(1, prime)]
    conference = np.zeros((prime + 1, prime + 1))
    conference[0, 1:] = 1.0
    conference[1:, 0] = 1.0
    for row_number in range(prime):
        for col_number in range(prime):
            offset = (col_number - row_number) % prime
            if offset != 0:
                conference[row_number + 1, col_number + 1] = 1.0 if offset in residues else -1.0
    first_block = np.array([[1.0, -1.0], [-1.0, -1.0]])
    second_block = np.array([[1.0, 1.0], [1.0, -1.0]])
    return np.kron(conference, first_block) + np.kron(np.eye(prime + 1), second_block)


def sylvester_table(order):
    result = np.ones((1, 1))
    while result.shape[0] < order:
        result = np.kron(np.array([[1.0, 1.0], [1.0, -1.0]]), result)
    return result


def rotary(values, positions):
    half_width = values.shape[-1] // 2
    frequency = ROPE_BASE ** (-2.0 * jnp.arange(half_width, dtype=jnp.float32) / values.shape[-1])
    angles = positions.astype(jnp.float32)[:, None] * frequency[None, :]
    cosine = jnp.cos(angles)
    sine = jnp.sin(angles)
    front = values[..., :half_width]
    back = values[..., half_width:]
    return jnp.concatenate([front * cosine - back * sine, back * cosine + front * sine], axis=-1)


def per_device(hidden, w_qkv, key_cache, value_cache, lengths, w_out, w_gate, w_up, w_down):
    row_count = hidden.shape[0]
    devices = lax.axis_size("tensor")
    device_index = lax.axis_index("tensor")
    query_width = H * HD
    kv_width = KVH * HD
    group_size = H // KVH
    score_scale = HD ** (-0.5)
    hidden_wide = hidden.astype(jnp.float32)
    squares = jnp.sum(hidden_wide * hidden_wide, axis=1)
    partial_sums = jnp.dot(hidden, w_qkv, preferred_element_type=jnp.float32)
    blocks = H + 2 * KVH
    rows_used = (blocks + 1) * row_count
    rows_sent = -(-rows_used // (8 * devices)) * 8
    stacked = jnp.concatenate(
        [
            partial_sums.reshape(row_count, blocks, HD).transpose(1, 0, 2).reshape(-1, HD),
            jnp.broadcast_to(squares[:, None], (row_count, HD)),
            jnp.zeros((rows_sent * devices - rows_used, HD), jnp.float32),
        ]
    ).astype(jnp.bfloat16)
    projected = gathered(scattered_sum(stacked.reshape(devices, rows_sent, HD)).astype(jnp.bfloat16))
    projected = projected.reshape(-1, HD)[:rows_used].astype(jnp.float32)
    projected = projected.reshape(blocks + 1, row_count, HD)
    inverse = lax.rsqrt(projected[blocks] / D + EPSILON)
    qkv = (projected[:blocks] * inverse).astype(jnp.bfloat16)
    turned = rotary(qkv[: H + KVH].astype(jnp.float32), lengths).astype(jnp.bfloat16)
    grouped = turned[:H].reshape(KVH, group_size, row_count, HD)
    keys_new = turned[H:]
    values_new = qkv[H + KVH :]
    local_length = key_cache.shape[1]
    positions = device_index * local_length + jnp.arange(local_length)
    live_mask = positions[None, :] < lengths[:, None]
    keys_local = key_cache.reshape(row_count, local_length, KVH, HD)
    values_local = value_cache.reshape(row_count, local_length, KVH, HD)
    scores = (
        jnp.einsum("kgrd,rckd->rkgc", grouped, keys_local, preferred_element_type=jnp.float32)
        * score_scale
    )
    weights = jnp.where(live_mask[:, None, None, :], jnp.exp(scores), jnp.float32(0.0))
    totals = jnp.sum(weights, axis=3)
    summed = jnp.einsum(
        "rkgc,rckd->rkgd",
        weights.astype(jnp.bfloat16),
        values_local,
        preferred_element_type=jnp.float32,
    )
    own_scores = (
        jnp.einsum("kgrd,krd->rkg", grouped, keys_new, preferred_element_type=jnp.float32)
        * score_scale
    )
    own_weights = jnp.where(device_index == 0, jnp.exp(own_scores), jnp.float32(0.0))
    totals = totals + own_weights
    summed = summed + own_weights[..., None] * values_new.astype(jnp.float32).transpose(1, 0, 2)[:, :, None, :]
    held = H * row_count // devices
    numerators = summed.transpose(1, 2, 0, 3).reshape(devices, held, HD)
    totals = totals.transpose(1, 2, 0).reshape(devices, 1, held)
    totals = jnp.pad(totals, ((0, 0), (0, 0), (0, HD - held)))
    parts = scattered_sum(jnp.concatenate([numerators, totals], axis=1).astype(jnp.bfloat16))
    piece = (parts[:held] / parts[held, :held][:, None]).astype(jnp.bfloat16)
    attention = gathered(piece).reshape(H, row_count, HD).transpose(1, 0, 2).reshape(row_count, query_width)
    residual = (hidden_wide + jnp.dot(attention, w_out, preferred_element_type=jnp.float32)).astype(
        jnp.bfloat16
    )
    residual_full = gathered(residual).transpose(1, 0, 2).reshape(row_count, D)
    residual_wide = residual_full.astype(jnp.float32)
    normed = (
        residual_wide
        * lax.rsqrt(jnp.mean(residual_wide * residual_wide, axis=1, keepdims=True) + EPSILON)
    ).astype(jnp.bfloat16)
    gate = jnp.dot(normed, w_gate, preferred_element_type=jnp.float32)
    upward = jnp.dot(normed, w_up, preferred_element_type=jnp.float32)
    activation = jax.nn.silu(gate) * upward
    local_width = activation.shape[1]
    local_table = jnp.asarray(
        np.kron(sylvester_table(local_width // 28), paley_table()), dtype=jnp.float32
    )
    mixed = jnp.dot(activation, local_table, precision=lax.Precision.HIGHEST)
    share = mixed.astype(jnp.bfloat16).reshape(devices, -1)
    share = lax.all_to_all(share, "tensor", 0, 0, tiled=True)
    share = jnp.dot(jnp.asarray(sylvester_table(devices), dtype=jnp.bfloat16), share, preferred_element_type=jnp.float32)
    share = lax.all_to_all((share * FF ** (-0.5)).astype(jnp.bfloat16), "tensor", 0, 0, tiled=True)
    rotated = share.reshape(row_count, local_width)
    down = jnp.dot(rotated, w_down, preferred_element_type=jnp.float32).astype(jnp.bfloat16)
    down_share = scattered_sum(down.reshape(row_count, devices, -1).transpose(1, 0, 2))
    return (residual.astype(jnp.float32) + down_share).astype(jnp.bfloat16)


def solution(mesh):
    in_specs = (
        P("groups", "tensor"),
        P("tensor", None),
        P("groups", "tensor", None),
        P("groups", "tensor", None),
        P("groups"),
        P(None, "tensor"),
        P(None, "tensor"),
        P(None, "tensor"),
        P("tensor", None),
    )
    out_specs = P("groups", "tensor")
    return jax.shard_map(
        per_device, mesh=mesh, in_specs=in_specs, out_specs=out_specs, check_vma=False
    )
```

```python
import jax
import jax.numpy as jnp
import numpy as np
from jax import lax
from jax.sharding import PartitionSpec as P

D = 8192
FF = 14336
H = 32
KVH = 4
HD = 128


EPSILON = 1e-05
ROPE_BASE = 500000.0


def across(value, apart):
    pairs = [(source, source ^ apart) for source in range(lax.axis_size("tensor"))]
    return lax.ppermute(value, "tensor", pairs)


def same_core():
    devices = lax.axis_size("tensor")
    return [list(range(core, devices, 2)) for core in range(2)]


def scattered_sum(pieces):
    second = lax.axis_index("tensor") % 2 == 1
    halves = pieces.reshape(-1, 2, *pieces.shape[1:])
    kept = jnp.where(second, halves[:, 1], halves[:, 0])
    sent = jnp.where(second, halves[:, 0], halves[:, 1]).astype(jnp.bfloat16)
    joined = kept.astype(jnp.float32) + across(sent, 1).astype(jnp.float32)
    received = lax.all_to_all(
        joined.astype(jnp.bfloat16), "tensor", 0, 0, tiled=True, axis_index_groups=same_core()
    )
    return jnp.sum(received.astype(jnp.float32), axis=0)


def gathered(piece):
    second = lax.axis_index("tensor") % 2 == 1
    copies = jnp.broadcast_to(piece[None], (lax.axis_size("tensor") // 2, *piece.shape))
    mine = lax.all_to_all(copies, "tensor", 0, 0, tiled=True, axis_index_groups=same_core())
    theirs = across(mine, 1)
    both = jnp.stack([jnp.where(second, theirs, mine), jnp.where(second, mine, theirs)], axis=1)
    return both.reshape(-1, *piece.shape)


def signed_pair(value, apart):
    upper = lax.axis_index("tensor") // apart % 2 == 1
    partner = across(value, apart).astype(jnp.float32)
    own = value.astype(jnp.float32)
    return jnp.where(upper, partner - own, own + partner)


def signed_sum(value):
    devices = lax.axis_size("tensor")
    middle = devices // 4
    groups = [
        [top * devices // 2 + 2 * inner + core for inner in range(middle)]
        for top in range(2)
        for core in range(2)
    ]
    value = signed_pair(value, 1)
    value = signed_pair(value.astype(jnp.bfloat16), devices // 2).astype(jnp.bfloat16)
    copies = jnp.broadcast_to(value[None], (middle, *value.shape))
    received = lax.all_to_all(copies, "tensor", 0, 0, tiled=True, axis_index_groups=groups)
    table = jnp.asarray(sylvester_table(middle), dtype=jnp.float32)
    signs = table[lax.axis_index("tensor") // 2 % middle]
    return jnp.sum(received.astype(jnp.float32) * signs[:, None, None], axis=0)


def paley_table():
    prime = 13
    residues = [value * value % prime for value in range(1, prime)]
    conference = np.zeros((prime + 1, prime + 1))
    conference[0, 1:] = 1.0
    conference[1:, 0] = 1.0
    for row_number in range(prime):
        for col_number in range(prime):
            offset = (col_number - row_number) % prime
            if offset != 0:
                conference[row_number + 1, col_number + 1] = 1.0 if offset in residues else -1.0
    first_block = np.array([[1.0, -1.0], [-1.0, -1.0]])
    second_block = np.array([[1.0, 1.0], [1.0, -1.0]])
    return np.kron(conference, first_block) + np.kron(np.eye(prime + 1), second_block)


def sylvester_table(order):
    result = np.ones((1, 1))
    while result.shape[0] < order:
        result = np.kron(np.array([[1.0, 1.0], [1.0, -1.0]]), result)
    return result


def rotary(values, positions):
    half_width = values.shape[-1] // 2
    frequency = ROPE_BASE ** (-2.0 * jnp.arange(half_width, dtype=jnp.float32) / values.shape[-1])
    angles = positions.astype(jnp.float32)[:, None] * frequency[None, :]
    cosine = jnp.cos(angles)
    sine = jnp.sin(angles)
    front = values[..., :half_width]
    back = values[..., half_width:]
    return jnp.concatenate([front * cosine - back * sine, back * cosine + front * sine], axis=-1)


def per_device(hidden, w_qkv, key_cache, value_cache, lengths, w_out, w_gate, w_up, w_down):
    row_count = hidden.shape[0]
    devices = lax.axis_size("tensor")
    device_index = lax.axis_index("tensor")
    query_width = H * HD
    kv_width = KVH * HD
    group_size = H // KVH
    score_scale = HD ** (-0.5)
    hidden_wide = hidden.astype(jnp.float32)
    squares = jnp.sum(hidden_wide * hidden_wide, axis=1)
    partial_sums = jnp.dot(hidden, w_qkv, preferred_element_type=jnp.float32)
    blocks = H + 2 * KVH
    rows_used = (blocks + 1) * row_count
    rows_sent = -(-rows_used // (8 * devices)) * 8
    stacked = jnp.concatenate(
        [
            partial_sums.reshape(row_count, blocks, HD).transpose(1, 0, 2).reshape(-1, HD),
            jnp.broadcast_to(squares[:, None], (row_count, HD)),
            jnp.zeros((rows_sent * devices - rows_used, HD), jnp.float32),
        ]
    ).astype(jnp.bfloat16)
    projected = gathered(scattered_sum(stacked.reshape(devices, rows_sent, HD)).astype(jnp.bfloat16))
    projected = projected.reshape(-1, HD)[:rows_used].astype(jnp.float32)
    projected = projected.reshape(blocks + 1, row_count, HD)
    inverse = lax.rsqrt(projected[blocks] / D + EPSILON)
    qkv = (projected[:blocks] * inverse).astype(jnp.bfloat16)
    turned = rotary(qkv[: H + KVH].astype(jnp.float32), lengths).astype(jnp.bfloat16)
    grouped = turned[:H].reshape(KVH, group_size, row_count, HD)
    keys_new = turned[H:]
    values_new = qkv[H + KVH :]
    local_length = key_cache.shape[1]
    positions = device_index * local_length + jnp.arange(local_length)
    live_mask = positions[None, :] < lengths[:, None]
    keys_local = key_cache.reshape(row_count, local_length, KVH, HD)
    values_local = value_cache.reshape(row_count, local_length, KVH, HD)
    scores = (
        jnp.einsum("kgrd,rckd->rkgc", grouped, keys_local, preferred_element_type=jnp.float32)
        * score_scale
    )
    weights = jnp.where(live_mask[:, None, None, :], jnp.exp(scores), jnp.float32(0.0))
    totals = jnp.sum(weights, axis=3)
    summed = jnp.einsum(
        "rkgc,rckd->rkgd",
        weights.astype(jnp.bfloat16),
        values_local,
        preferred_element_type=jnp.float32,
    )
    own_scores = (
        jnp.einsum("kgrd,krd->rkg", grouped, keys_new, preferred_element_type=jnp.float32)
        * score_scale
    )
    own_weights = jnp.where(device_index == 0, jnp.exp(own_scores), jnp.float32(0.0))
    totals = totals + own_weights
    summed = summed + own_weights[..., None] * values_new.astype(jnp.float32).transpose(1, 0, 2)[:, :, None, :]
    held = H * row_count // devices
    numerators = summed.transpose(1, 2, 0, 3).reshape(devices, held, HD)
    totals = totals.transpose(1, 2, 0).reshape(devices, 1, held)
    totals = jnp.pad(totals, ((0, 0), (0, 0), (0, HD - held)))
    parts = scattered_sum(jnp.concatenate([numerators, totals], axis=1).astype(jnp.bfloat16))
    piece = (parts[:held] / parts[held, :held][:, None]).astype(jnp.bfloat16)
    attention = gathered(piece).reshape(H, row_count, HD).transpose(1, 0, 2).reshape(row_count, query_width)
    residual = (hidden_wide + jnp.dot(attention, w_out, preferred_element_type=jnp.float32)).astype(
        jnp.bfloat16
    )
    residual_full = gathered(residual).transpose(1, 0, 2).reshape(row_count, D)
    residual_wide = residual_full.astype(jnp.float32)
    normed = (
        residual_wide
        * lax.rsqrt(jnp.mean(residual_wide * residual_wide, axis=1, keepdims=True) + EPSILON)
    ).astype(jnp.bfloat16)
    gate = jnp.dot(normed, w_gate, preferred_element_type=jnp.float32)
    upward = jnp.dot(normed, w_up, preferred_element_type=jnp.float32)
    activation = jax.nn.silu(gate) * upward
    local_width = activation.shape[1]
    local_table = jnp.asarray(
        np.kron(sylvester_table(local_width // 28), paley_table()), dtype=jnp.float32
    )
    mixed = jnp.dot(activation, local_table, precision=lax.Precision.HIGHEST)
    rotated = (signed_sum(mixed) * FF ** (-0.5)).astype(jnp.bfloat16)
    down = jnp.dot(rotated, w_down, preferred_element_type=jnp.float32).astype(jnp.bfloat16)
    down_share = scattered_sum(down.reshape(row_count, devices, -1).transpose(1, 0, 2))
    return (residual.astype(jnp.float32) + down_share).astype(jnp.bfloat16)


def solution(mesh):
    in_specs = (
        P("groups", "tensor"),
        P("tensor", None),
        P("groups", "tensor", None),
        P("groups", "tensor", None),
        P("groups"),
        P(None, "tensor"),
        P(None, "tensor"),
        P(None, "tensor"),
        P("tensor", None),
    )
    out_specs = P("groups", "tensor")
    return jax.shard_map(
        per_device, mesh=mesh, in_specs=in_specs, out_specs=out_specs, check_vma=False
    )
```

```python
import jax
import jax.numpy as jnp
import numpy as np
from jax import lax
from jax.experimental import pallas as pl
from jax.experimental.pallas import tpu as pltpu
from jax.sharding import PartitionSpec as P

D = 8192
FF = 14336
H = 32
KVH = 4
HD = 128


EPSILON = 1e-05
ROPE_BASE = 500000.0
QKV_CHUNK = 1024
DOWN_CHUNK = 1024
ROW_CHUNK = 4
ROWS_AT_ONCE = 8


def across(value, apart):
    pairs = [(source, source ^ apart) for source in range(lax.axis_size("tensor"))]
    return lax.ppermute(value, "tensor", pairs)


def same_core():
    devices = lax.axis_size("tensor")
    return [list(range(core, devices, 2)) for core in range(2)]


def scattered_sum(pieces):
    second = lax.axis_index("tensor") % 2 == 1
    halves = pieces.reshape(-1, 2, *pieces.shape[1:])
    kept = jnp.where(second, halves[:, 1], halves[:, 0])
    sent = jnp.where(second, halves[:, 0], halves[:, 1]).astype(jnp.bfloat16)
    return scattered_halves(kept, sent)


def scattered_halves(kept, sent):
    return scattered_joined(kept, across(sent, 1))


def scattered_joined(kept, arrived):
    joined = kept.astype(jnp.float32) + arrived.astype(jnp.float32)
    received = lax.all_to_all(
        joined.astype(jnp.bfloat16), "tensor", 0, 0, tiled=True, axis_index_groups=same_core()
    )
    return jnp.sum(received.astype(jnp.float32), axis=0)


def gathered(piece):
    second = lax.axis_index("tensor") % 2 == 1
    copies = jnp.broadcast_to(piece[None], (lax.axis_size("tensor") // 2, *piece.shape))
    mine = lax.all_to_all(copies, "tensor", 0, 0, tiled=True, axis_index_groups=same_core())
    theirs = across(mine, 1)
    both = jnp.stack([jnp.where(second, theirs, mine), jnp.where(second, mine, theirs)], axis=1)
    return both.reshape(-1, *piece.shape)


def signed_pair(value, apart):
    upper = lax.axis_index("tensor") // apart % 2 == 1
    partner = across(value, apart).astype(jnp.float32)
    own = value.astype(jnp.float32)
    return jnp.where(upper, partner - own, own + partner)


def signed_sum(value):
    devices = lax.axis_size("tensor")
    middle = devices // 4
    groups = [
        [top * devices // 2 + 2 * inner + core for inner in range(middle)]
        for top in range(2)
        for core in range(2)
    ]
    value = signed_pair(value, 1)
    value = signed_pair(value.astype(jnp.bfloat16), devices // 2).astype(jnp.bfloat16)
    copies = jnp.broadcast_to(value[None], (middle, *value.shape))
    received = lax.all_to_all(copies, "tensor", 0, 0, tiled=True, axis_index_groups=groups)
    received, index = lax.optimization_barrier((received, lax.axis_index("tensor")))
    common = jnp.arange(middle) & (index // 2 % middle)
    for shift in (4, 2, 1):
        common = common ^ (common >> shift)
    signs = 1.0 - 2.0 * (common & 1).astype(jnp.float32)
    return jnp.sum(received.astype(jnp.float32) * signs[:, None, None], axis=0)


def in_hbm(value):
    return pltpu.with_memory_space_constraint(value, pltpu.HBM)


def column_copies(weights_ref, held_ref, arrived, chunk):
    copies = []
    for start in range(0, weights_ref.shape[1], chunk):
        part = (slice(None), pl.ds(start, chunk))
        copies.append(
            pltpu.make_async_copy(
                weights_ref.at[part], held_ref.at[part], arrived.at[start // chunk]
            )
        )
        copies[-1].start()
    return copies


def project_kernel(
    core_ref, hidden_source, source_ref, out_ref, hidden_ref, hidden_arrived, weights_ref, arrived, stacked
):
    hidden_copy = pltpu.make_async_copy(hidden_source, hidden_ref, hidden_arrived)
    hidden_copy.start()
    copies = column_copies(source_ref, weights_ref, arrived, QKV_CHUNK)
    core = core_ref[0]
    rows = hidden_ref.shape[0]
    columns = weights_ref.shape[1]
    hidden_copy.wait()
    hidden = hidden_ref[...]
    wide = hidden.astype(jnp.float32)
    squares = jnp.sum(wide * wide, axis=1, keepdims=True)
    for start in range(0, columns, 2 * HD):
        if start % QKV_CHUNK == 0:
            copies[start // QKV_CHUNK].wait()
        part = jnp.dot(
            hidden, weights_ref[:, start : start + 2 * HD], preferred_element_type=jnp.float32
        )
        first = start // HD * rows
        stacked[first : first + rows] = part[:, :HD]
        stacked[first + rows : first + 2 * rows] = part[:, HD:]
    used = columns // HD * rows
    stacked[used : used + rows] = jnp.broadcast_to(squares, (rows, HD))
    stacked[used + rows :] = jnp.zeros((stacked.shape[0] - used - rows, HD), jnp.float32)
    held = out_ref.shape[2]
    for piece in range(stacked.shape[0] // held):
        values = stacked[piece * held : (piece + 1) * held].astype(jnp.bfloat16)
        out_ref[(piece % 2) ^ core, piece // 2] = values


def projected_pieces(core, hidden, w_qkv, devices, rows_sent):
    vmem = pl.BlockSpec(memory_space=pltpu.VMEM)
    return pl.pallas_call(
        project_kernel,
        out_shape=jax.ShapeDtypeStruct((2, devices // 2, rows_sent, HD), jnp.bfloat16),
        in_specs=[
            pl.BlockSpec(memory_space=pltpu.SMEM),
            pl.BlockSpec(memory_space=pltpu.HBM),
            pl.BlockSpec(memory_space=pltpu.HBM),
        ],
        out_specs=vmem,
        scratch_shapes=[
            pltpu.VMEM(hidden.shape, hidden.dtype),
            pltpu.SemaphoreType.DMA,
            pltpu.VMEM(w_qkv.shape, w_qkv.dtype),
            pltpu.SemaphoreType.DMA((w_qkv.shape[1] // QKV_CHUNK,)),
            pltpu.VMEM((devices * rows_sent, HD), jnp.float32),
        ],
        compiler_params=pltpu.CompilerParams(vmem_limit_bytes=8 * 2**20),
        cost_estimate=pl.CostEstimate(
            flops=2 * hidden.shape[0] * w_qkv.size, bytes_accessed=2 * w_qkv.size, transcendentals=0
        ),
    )(core, in_hbm(hidden), in_hbm(w_qkv))


def attend_kernel(
    device_ref, core_ref, lengths_ref, projected_ref, cosine_ref, sine_ref, key_source, value_source,
    out_ref, keys_ref, values_ref, keys_arrived, values_arrived, queries, fresh, sums,
):
    rows, slots = keys_ref.shape[0], keys_ref.shape[1]

    def copies(index):
        part = pl.ds(index * ROW_CHUNK, ROW_CHUNK)
        return (
            pltpu.make_async_copy(key_source.at[part], keys_ref.at[part], keys_arrived.at[index]),
            pltpu.make_async_copy(value_source.at[part], values_ref.at[part], values_arrived.at[index]),
        )

    for index in range(rows // ROW_CHUNK):
        for copy in copies(index):
            copy.start()
    device, core = device_ref[0], core_ref[0]
    group = H // KVH
    scale = HD ** (-0.5)
    cosine, sine = cosine_ref[...], sine_ref[...]
    inverse = lax.rsqrt(projected_ref[H + 2 * KVH].astype(jnp.float32) / D + EPSILON)

    def block(index):
        value = projected_ref[index].astype(jnp.float32) * inverse
        return value.astype(jnp.bfloat16).astype(jnp.float32)

    def turned(index):
        value = block(index)
        value = value * cosine + pltpu.roll(value, HD // 2, 1) * sine
        return value.astype(jnp.bfloat16).astype(jnp.float32)

    for head in range(H):
        queries[pl.ds(head, rows, stride=H), :] = turned(head)
    for head in range(KVH):
        fresh[pl.ds(head, rows, stride=2 * KVH), :] = turned(H + head)
        fresh[pl.ds(KVH + head, rows, stride=2 * KVH), :] = block(H + KVH + head)

    lane = lax.broadcasted_iota(jnp.int32, (1, slots), 1) + device * slots
    row_lane = lax.broadcasted_iota(jnp.int32, (H, HD), 1)
    pair_row = lax.broadcasted_iota(jnp.int32, (2 * group, HD), 0)
    lower = pair_row < group
    pairs = KVH // 2

    def expand(first):
        picked = [
            jnp.broadcast_to(fresh[pl.ds(first + head, 1), :], (group, HD)) for head in range(KVH)
        ]
        return jnp.concatenate(picked, axis=0)

    def some_rows(step, totals, count):
        numbers = [step * count + offset for offset in range(count)]
        scores = []
        own = []
        for offset, row in enumerate(numbers):
            if offset % ROW_CHUNK == 0:
                copies(step * (count // ROW_CHUNK) + offset // ROW_CHUNK)[0].wait()
            query = queries[pl.ds(pl.multiple_of(row * H, H), H), :]
            own_score = jnp.sum(query * expand(row * 2 * KVH), axis=1, keepdims=True) * scale
            own.append(jnp.where(device == 0, jnp.exp(own_score), 0.0))
            parts = []
            for pair in range(pairs):
                chosen = query[pair * 2 * group : (pair + 1) * 2 * group]
                spread = jnp.concatenate(
                    [jnp.where(lower, chosen, 0.0), jnp.where(lower, 0.0, chosen)], axis=1
                ).astype(jnp.bfloat16)
                parts.append(
                    lax.dot_general(
                        spread,
                        keys_ref[row, :, pair * 2 * HD : (pair + 1) * 2 * HD],
                        (((1,), (1,)), ((), ())),
                        preferred_element_type=jnp.float32,
                    )
                )
            scores.append(jnp.concatenate(parts, axis=0))
        weights = [
            jnp.where(lane < lengths_ref[pl.ds(row, 1), :1], jnp.exp(score * scale), 0.0)
            for row, score in zip(numbers, scores)
        ]
        for offset, (row, weight, own_weight) in enumerate(zip(numbers, weights, own)):
            if offset % ROW_CHUNK == 0:
                copies(step * (count // ROW_CHUNK) + offset // ROW_CHUNK)[1].wait()
            rounded = weight.astype(jnp.bfloat16)
            parts = []
            for pair in range(pairs):
                product = jnp.dot(
                    rounded[pair * 2 * group : (pair + 1) * 2 * group],
                    values_ref[row, :, pair * 2 * HD : (pair + 1) * 2 * HD],
                    preferred_element_type=jnp.float32,
                )
                parts.append(product[:group, :HD])
                parts.append(product[group:, HD:])
            total = jnp.sum(weight, axis=1, keepdims=True) + own_weight
            summed = jnp.concatenate(parts, axis=0) + own_weight * expand(row * 2 * KVH + KVH)
            sums[pl.ds(pl.multiple_of(row * H, H), H), :] = summed
            totals = jnp.where(row_lane == row, total, totals)
        return totals

    count = ROWS_AT_ONCE
    totals = lax.fori_loop(
        0,
        rows // count,
        lambda step, totals: some_rows(step, totals, count),
        jnp.zeros((H, HD), jnp.float32),
    )
    for head in range(H):
        start = head // 8 * 8
        values = jnp.concatenate(
            [sums[pl.ds(head, rows, stride=H), :], totals[start : start + 8]], axis=0
        )
        out_ref[(head % 2) ^ core, head // 2] = values.astype(jnp.bfloat16)


def attended_pieces(device, core, lengths, projected, cosine, sine, key_cache, value_cache):
    rows, slots = key_cache.shape[0], key_cache.shape[1]
    smem = pl.BlockSpec(memory_space=pltpu.SMEM)
    vmem = pl.BlockSpec(memory_space=pltpu.VMEM)
    return pl.pallas_call(
        attend_kernel,
        out_shape=jax.ShapeDtypeStruct((2, H // 2, rows + 8, HD), jnp.bfloat16),
        in_specs=[smem] * 2 + [vmem] * 4 + [pl.BlockSpec(memory_space=pltpu.HBM)] * 2,
        out_specs=vmem,
        scratch_shapes=[
            pltpu.VMEM(key_cache.shape, key_cache.dtype),
            pltpu.VMEM(value_cache.shape, value_cache.dtype),
            pltpu.SemaphoreType.DMA((rows // ROW_CHUNK,)),
            pltpu.SemaphoreType.DMA((rows // ROW_CHUNK,)),
            pltpu.VMEM((rows * H, HD), jnp.float32),
            pltpu.VMEM((rows * 2 * KVH, HD), jnp.float32),
            pltpu.VMEM((rows * H, HD), jnp.float32),
        ],
        compiler_params=pltpu.CompilerParams(vmem_limit_bytes=20 * 2**20),
        cost_estimate=pl.CostEstimate(
            flops=4 * rows * H * slots * HD,
            bytes_accessed=2 * (key_cache.size + value_cache.size),
            transcendentals=rows * H * slots,
        ),
    )(device, core, lengths, projected, cosine, sine, in_hbm(key_cache), in_hbm(value_cache))


def down_kernel(core_ref, rotated_ref, source_ref, out_ref, weights_ref, arrived):
    copies = column_copies(source_ref, weights_ref, arrived, DOWN_CHUNK)
    core = core_ref[0]
    rotated = rotated_ref[...]
    features = weights_ref.shape[1]
    width = out_ref.shape[3]
    block = max(width, min(256, features))
    for start in range(0, features, block):
        if start % DOWN_CHUNK == 0:
            copies[start // DOWN_CHUNK].wait()
        part = jnp.dot(
            rotated, weights_ref[:, start : start + block], preferred_element_type=jnp.float32
        ).astype(jnp.bfloat16)
        for offset in range(0, block, width):
            piece = (start + offset) // width
            out_ref[(piece % 2) ^ core, piece // 2] = part[:, offset : offset + width]


def down_pieces(core, rotated, w_down, devices):
    rows, features = rotated.shape[0], w_down.shape[1]
    vmem = pl.BlockSpec(memory_space=pltpu.VMEM)
    return pl.pallas_call(
        down_kernel,
        out_shape=jax.ShapeDtypeStruct((2, devices // 2, rows, features // devices), jnp.bfloat16),
        in_specs=[
            pl.BlockSpec(memory_space=pltpu.SMEM),
            vmem,
            pl.BlockSpec(memory_space=pltpu.HBM),
        ],
        out_specs=vmem,
        scratch_shapes=[
            pltpu.VMEM(w_down.shape, w_down.dtype),
            pltpu.SemaphoreType.DMA((w_down.shape[1] // DOWN_CHUNK,)),
        ],
        compiler_params=pltpu.CompilerParams(vmem_limit_bytes=12 * 2**20),
        cost_estimate=pl.CostEstimate(
            flops=2 * rows * rotated.shape[1] * features,
            bytes_accessed=w_down.size * 2,
            transcendentals=0,
        ),
    )(core, rotated, in_hbm(w_down))


def paley_table():
    prime = 13
    residues = [value * value % prime for value in range(1, prime)]
    conference = np.zeros((prime + 1, prime + 1))
    conference[0, 1:] = 1.0
    conference[1:, 0] = 1.0
    for row_number in range(prime):
        for col_number in range(prime):
            offset = (col_number - row_number) % prime
            if offset != 0:
                conference[row_number + 1, col_number + 1] = 1.0 if offset in residues else -1.0
    first_block = np.array([[1.0, -1.0], [-1.0, -1.0]])
    second_block = np.array([[1.0, 1.0], [1.0, -1.0]])
    return np.kron(conference, first_block) + np.kron(np.eye(prime + 1), second_block)


def sylvester_table(order):
    result = np.ones((1, 1))
    while result.shape[0] < order:
        result = np.kron(np.array([[1.0, 1.0], [1.0, -1.0]]), result)
    return result


def rotary_factors(positions):
    frequency = ROPE_BASE ** (-2.0 * jnp.arange(HD // 2, dtype=jnp.float32) / HD)
    angles = positions.astype(jnp.float32)[:, None] * frequency[None, :]
    cosine, sine = jnp.cos(angles), jnp.sin(angles)
    return jnp.concatenate([cosine, cosine], axis=1), jnp.concatenate([-sine, sine], axis=1)


def per_device(hidden, w_qkv, key_cache, value_cache, lengths, w_out, w_gate, w_up, w_down):
    row_count = hidden.shape[0]
    devices = lax.axis_size("tensor")
    device_index = lax.axis_index("tensor")
    query_width = H * HD
    device = device_index.astype(jnp.int32).reshape(1)
    core = device % 2
    hidden_wide = hidden.astype(jnp.float32)
    blocks = H + 2 * KVH
    rows_used = (blocks + 1) * row_count
    rows_sent = -(-rows_used // (8 * devices)) * 8
    halves = projected_pieces(core, hidden, w_qkv, devices, rows_sent)
    halves, lengths = lax.optimization_barrier((halves, lengths))
    arrived = across(halves[1], 1)
    cosine, sine = rotary_factors(lengths)
    lengths = jnp.broadcast_to(lengths[:, None], (row_count, HD))
    arrived, cosine, sine, lengths = lax.optimization_barrier((arrived, cosine, sine, lengths))
    piece = scattered_joined(halves[0], arrived).astype(jnp.bfloat16)
    projected = gathered(piece)
    projected = projected.reshape(-1, HD)[:rows_used].reshape(blocks + 1, row_count, HD)
    direct = devices == H
    halves = attended_pieces(
        device, core if direct else jnp.zeros_like(core), lengths, projected, cosine, sine, key_cache, value_cache
    )
    if direct:
        parts = scattered_halves(halves[0], halves[1])
        parts, device_index = lax.optimization_barrier((parts, device_index))
        numerators, totals = parts[:row_count], parts[row_count:]
        chosen = jnp.arange(8) == device_index % 8
        totals = jnp.sum(jnp.where(chosen[:, None], totals, 0.0), axis=0)[:row_count]
    else:
        held = H * row_count // devices
        heads = halves.transpose(1, 0, 2, 3).reshape(H, row_count + 8, HD)
        numerators = heads[:, :row_count].reshape(devices, held, HD)
        totals = heads[:, row_count:].reshape(H // 8, 8, 8, HD)
        totals = jnp.einsum("ahhl->ahl", totals).reshape(H, HD)[:, :row_count]
        totals = jnp.pad(totals.reshape(devices, 1, held), ((0, 0), (0, 0), (0, HD - held)))
        parts = scattered_sum(jnp.concatenate([numerators, totals], axis=1))
        numerators, totals = parts[:held], parts[held, :held]
    piece = (numerators / totals[:, None]).astype(jnp.bfloat16)
    attention = gathered(piece).reshape(H, row_count, HD).transpose(1, 0, 2).reshape(row_count, query_width)
    residual = (hidden_wide + jnp.dot(attention, w_out, preferred_element_type=jnp.float32)).astype(
        jnp.bfloat16
    )
    residual_full = gathered(residual).transpose(1, 0, 2).reshape(row_count, D)
    residual_wide = residual_full.astype(jnp.float32)
    normed = (
        residual_wide
        * lax.rsqrt(jnp.mean(residual_wide * residual_wide, axis=1, keepdims=True) + EPSILON)
    ).astype(jnp.bfloat16)
    gate = jnp.dot(normed, w_gate, preferred_element_type=jnp.float32)
    upward = jnp.dot(normed, w_up, preferred_element_type=jnp.float32)
    activation = jax.nn.silu(gate) * upward
    local_width = activation.shape[1]
    local_table = jnp.asarray(
        np.kron(sylvester_table(local_width // 28), paley_table()), dtype=jnp.float32
    )
    mixed = jnp.dot(activation, local_table, precision=lax.Precision.HIGHEST)
    rotated = (signed_sum(mixed) * FF ** (-0.5)).astype(jnp.bfloat16)
    halves = down_pieces(core, rotated, w_down, devices)
    down_share = scattered_halves(halves[0], halves[1])
    return (residual.astype(jnp.float32) + down_share).astype(jnp.bfloat16)


def solution(mesh):
    in_specs = (
        P("groups", "tensor"),
        P("tensor", None),
        P("groups", "tensor", None),
        P("groups", "tensor", None),
        P("groups"),
        P(None, "tensor"),
        P(None, "tensor"),
        P(None, "tensor"),
        P("tensor", None),
    )
    out_specs = P("groups", "tensor")
    return jax.shard_map(
        per_device, mesh=mesh, in_specs=in_specs, out_specs=out_specs, check_vma=False
    )
```

```python
import jax
import jax.numpy as jnp
import numpy as np
from jax import lax
from jax.experimental import pallas as pl
from jax.experimental.pallas import tpu as pltpu
from jax.sharding import PartitionSpec as P

D = 8192
FF = 14336
H = 32
KVH = 4
HD = 128


EPSILON = 1e-05
ROPE_BASE = 500000.0
QKV_CHUNK = 2560
DOWN_CHUNK = 1024
ROW_CHUNK = 8
ROWS_AT_ONCE = 8


def across(value, apart):
    pairs = [(source, source ^ apart) for source in range(lax.axis_size("tensor"))]
    return lax.ppermute(value, "tensor", pairs)


def same_core():
    devices = lax.axis_size("tensor")
    return [list(range(core, devices, 2)) for core in range(2)]


def scattered_sum(pieces):
    second = lax.axis_index("tensor") % 2 == 1
    halves = pieces.reshape(-1, 2, *pieces.shape[1:])
    kept = jnp.where(second, halves[:, 1], halves[:, 0])
    sent = jnp.where(second, halves[:, 0], halves[:, 1]).astype(jnp.bfloat16)
    return scattered_halves(kept, sent)


def scattered_halves(kept, sent):
    return scattered_joined(kept, across(sent, 1))


def scattered_joined(kept, arrived):
    joined = kept.astype(jnp.float32) + arrived.astype(jnp.float32)
    received = lax.all_to_all(
        joined.astype(jnp.bfloat16), "tensor", 0, 0, tiled=True, axis_index_groups=same_core()
    )
    return jnp.sum(received.astype(jnp.float32), axis=0)


def gathered_at_once(piece):
    copies = jnp.broadcast_to(piece[None], (lax.axis_size("tensor"), *piece.shape))
    return lax.all_to_all(copies, "tensor", 0, 0, tiled=True)


def gathered(piece):
    second = lax.axis_index("tensor") % 2 == 1
    copies = jnp.broadcast_to(piece[None], (lax.axis_size("tensor") // 2, *piece.shape))
    mine = lax.all_to_all(copies, "tensor", 0, 0, tiled=True, axis_index_groups=same_core())
    theirs = across(mine, 1)
    both = jnp.stack([jnp.where(second, theirs, mine), jnp.where(second, mine, theirs)], axis=1)
    return both.reshape(-1, *piece.shape)


def signed_pair(value, apart):
    upper = lax.axis_index("tensor") // apart % 2 == 1
    partner = across(value, apart).astype(jnp.float32)
    own = value.astype(jnp.float32)
    return jnp.where(upper, partner - own, own + partner)


def signed_sum(value):
    devices = lax.axis_size("tensor")
    middle = devices // 4
    groups = [
        [top * devices // 2 + 2 * inner + core for inner in range(middle)]
        for top in range(2)
        for core in range(2)
    ]
    value = signed_pair(value, 1)
    value = signed_pair(value.astype(jnp.bfloat16), devices // 2).astype(jnp.bfloat16)
    copies = jnp.broadcast_to(value[None], (middle, *value.shape))
    received = lax.all_to_all(copies, "tensor", 0, 0, tiled=True, axis_index_groups=groups)
    received, index = lax.optimization_barrier((received, lax.axis_index("tensor")))
    common = jnp.arange(middle) & (index // 2 % middle)
    for shift in (4, 2, 1):
        common = common ^ (common >> shift)
    signs = 1.0 - 2.0 * (common & 1).astype(jnp.float32)
    return jnp.sum(received.astype(jnp.float32) * signs[:, None, None], axis=0)


def normalize_kernel(device_ref, parts_ref, out_ref):
    rows = out_ref.shape[0]
    shape = (8, HD)
    chosen = lax.broadcasted_iota(jnp.int32, shape, 0) == device_ref[0] % 8
    totals = jnp.sum(jnp.where(chosen, parts_ref[rows : rows + 8], 0.0), axis=0, keepdims=True)
    shape = (rows, HD)
    own = lax.broadcasted_iota(jnp.int32, shape, 0) == lax.broadcasted_iota(jnp.int32, shape, 1)
    column = jnp.sum(jnp.where(own, totals, 0.0), axis=1, keepdims=True)
    out_ref[...] = (parts_ref[:rows] / column).astype(jnp.bfloat16)


def normalized(device, parts, rows):
    vmem = pl.BlockSpec(memory_space=pltpu.VMEM)
    return pl.pallas_call(
        normalize_kernel,
        out_shape=jax.ShapeDtypeStruct((rows, HD), jnp.bfloat16),
        in_specs=[pl.BlockSpec(memory_space=pltpu.SMEM), vmem],
        out_specs=vmem,
        compiler_params=pltpu.CompilerParams(vmem_limit_bytes=2**20),
        cost_estimate=pl.CostEstimate(flops=10000, bytes_accessed=10000, transcendentals=0),
    )(device, parts)


def in_hbm(value):
    return pltpu.with_memory_space_constraint(value, pltpu.HBM)


def column_copies(weights_ref, held_ref, arrived, chunk):
    copies = []
    for start in range(0, weights_ref.shape[1], chunk):
        part = (slice(None), pl.ds(start, chunk))
        copies.append(
            pltpu.make_async_copy(
                weights_ref.at[part], held_ref.at[part], arrived.at[start // chunk]
            )
        )
        copies[-1].start()
    return copies


def project_kernel(
    core_ref, hidden_source, source_ref, out_ref, hidden_ref, hidden_arrived, weights_ref, arrived, stacked
):
    hidden_copy = pltpu.make_async_copy(hidden_source, hidden_ref, hidden_arrived)
    hidden_copy.start()
    copies = column_copies(source_ref, weights_ref, arrived, QKV_CHUNK)
    core = core_ref[0]
    rows = hidden_ref.shape[0]
    columns = weights_ref.shape[1]
    hidden_copy.wait()
    hidden = hidden_ref[...]
    wide = hidden.astype(jnp.float32)
    squares = jnp.sum(wide * wide, axis=1, keepdims=True)
    for start in range(0, columns, 2 * HD):
        if start % QKV_CHUNK == 0:
            copies[start // QKV_CHUNK].wait()
        part = jnp.dot(
            hidden, weights_ref[:, start : start + 2 * HD], preferred_element_type=jnp.float32
        )
        first = start // HD * rows
        stacked[first : first + rows] = part[:, :HD]
        stacked[first + rows : first + 2 * rows] = part[:, HD:]
    used = columns // HD * rows
    stacked[used : used + rows] = jnp.broadcast_to(squares, (rows, HD))
    stacked[used + rows :] = jnp.zeros((stacked.shape[0] - used - rows, HD), jnp.float32)
    held = out_ref.shape[2]
    for piece in range(stacked.shape[0] // held):
        values = stacked[piece * held : (piece + 1) * held].astype(jnp.bfloat16)
        out_ref[(piece % 2) ^ core, piece // 2] = values


def projected_pieces(core, hidden, w_qkv, devices, rows_sent):
    vmem = pl.BlockSpec(memory_space=pltpu.VMEM)
    return pl.pallas_call(
        project_kernel,
        out_shape=jax.ShapeDtypeStruct((2, devices // 2, rows_sent, HD), jnp.bfloat16),
        in_specs=[
            pl.BlockSpec(memory_space=pltpu.SMEM),
            pl.BlockSpec(memory_space=pltpu.HBM),
            pl.BlockSpec(memory_space=pltpu.HBM),
        ],
        out_specs=vmem,
        scratch_shapes=[
            pltpu.VMEM(hidden.shape, hidden.dtype),
            pltpu.SemaphoreType.DMA,
            pltpu.VMEM(w_qkv.shape, w_qkv.dtype),
            pltpu.SemaphoreType.DMA((w_qkv.shape[1] // QKV_CHUNK,)),
            pltpu.VMEM((devices * rows_sent, HD), jnp.float32),
        ],
        compiler_params=pltpu.CompilerParams(vmem_limit_bytes=8 * 2**20),
        cost_estimate=pl.CostEstimate(
            flops=2 * hidden.shape[0] * w_qkv.size, bytes_accessed=2 * w_qkv.size, transcendentals=0
        ),
    )(core, in_hbm(hidden), in_hbm(w_qkv))


def attend_kernel(
    device_ref, core_ref, lengths_ref, projected_ref, cosine_ref, sine_ref, key_source, value_source,
    out_ref, keys_ref, values_ref, keys_arrived, values_arrived, queries, fresh, sums,
):
    rows, slots = keys_ref.shape[0], keys_ref.shape[1]

    def copies(index):
        part = pl.ds(index * ROW_CHUNK, ROW_CHUNK)
        return (
            pltpu.make_async_copy(key_source.at[part], keys_ref.at[part], keys_arrived.at[index]),
            pltpu.make_async_copy(value_source.at[part], values_ref.at[part], values_arrived.at[index]),
        )

    for index in range(rows // ROW_CHUNK):
        for copy in copies(index):
            copy.start()
    device, core = device_ref[0], core_ref[0]
    group = H // KVH
    scale = HD ** (-0.5)
    cosine, sine = cosine_ref[...], sine_ref[...]
    inverse = lax.rsqrt(projected_ref[H + 2 * KVH].astype(jnp.float32) / D + EPSILON)

    def block(index):
        value = projected_ref[index].astype(jnp.float32) * inverse
        return value.astype(jnp.bfloat16).astype(jnp.float32)

    def turned(index):
        value = block(index)
        value = value * cosine + pltpu.roll(value, HD // 2, 1) * sine
        return value.astype(jnp.bfloat16).astype(jnp.float32)

    for head in range(H):
        queries[pl.ds(head, rows, stride=H), :] = turned(head)
    for head in range(KVH):
        fresh[pl.ds(head, rows, stride=2 * KVH), :] = turned(H + head)
        fresh[pl.ds(KVH + head, rows, stride=2 * KVH), :] = block(H + KVH + head)

    lane = lax.broadcasted_iota(jnp.int32, (1, slots), 1) + device * slots
    lane = lane.astype(jnp.float32)
    row_lane = lax.broadcasted_iota(jnp.int32, (H, HD), 1)
    pair_row = lax.broadcasted_iota(jnp.int32, (2 * group, HD), 0)
    lower = pair_row < group
    pairs = KVH // 2

    def expand(first):
        picked = [
            jnp.broadcast_to(fresh[pl.ds(first + head, 1), :], (group, HD)) for head in range(KVH)
        ]
        return jnp.concatenate(picked, axis=0)

    def some_rows(step, totals, count):
        numbers = [step * count + offset for offset in range(count)]
        scores = []
        own = []
        for offset, row in enumerate(numbers):
            if offset % ROW_CHUNK == 0:
                copies(step * (count // ROW_CHUNK) + offset // ROW_CHUNK)[0].wait()
            query = queries[pl.ds(pl.multiple_of(row * H, H), H), :]
            own_score = jnp.sum(query * expand(row * 2 * KVH), axis=1, keepdims=True) * scale
            own.append(jnp.where(device == 0, jnp.exp(own_score), 0.0))
            parts = []
            for pair in range(pairs):
                chosen = query[pair * 2 * group : (pair + 1) * 2 * group]
                spread = jnp.concatenate(
                    [jnp.where(lower, chosen, 0.0), jnp.where(lower, 0.0, chosen)], axis=1
                ).astype(jnp.bfloat16)
                parts.append(
                    lax.dot_general(
                        spread,
                        keys_ref[row, :, pair * 2 * HD : (pair + 1) * 2 * HD],
                        (((1,), (1,)), ((), ())),
                        preferred_element_type=jnp.float32,
                    )
                )
            scores.append(jnp.concatenate(parts, axis=0))
        weights = [
            jnp.where(lane < lengths_ref[pl.ds(row, 1), :1], jnp.exp(score * scale), 0.0)
            for row, score in zip(numbers, scores)
        ]
        for offset, (row, weight, own_weight) in enumerate(zip(numbers, weights, own)):
            if offset % ROW_CHUNK == 0:
                copies(step * (count // ROW_CHUNK) + offset // ROW_CHUNK)[1].wait()
            rounded = weight.astype(jnp.bfloat16)
            parts = []
            for pair in range(pairs):
                product = jnp.dot(
                    rounded[pair * 2 * group : (pair + 1) * 2 * group],
                    values_ref[row, :, pair * 2 * HD : (pair + 1) * 2 * HD],
                    preferred_element_type=jnp.float32,
                )
                parts.append(product[:group, :HD])
                parts.append(product[group:, HD:])
            total = jnp.sum(weight, axis=1, keepdims=True) + own_weight
            summed = jnp.concatenate(parts, axis=0) + own_weight * expand(row * 2 * KVH + KVH)
            sums[pl.ds(pl.multiple_of(row * H, H), H), :] = summed
            totals = jnp.where(row_lane == row, total, totals)
        return totals

    count = ROWS_AT_ONCE
    totals = lax.fori_loop(
        0,
        rows // count,
        lambda step, totals: some_rows(step, totals, count),
        jnp.zeros((H, HD), jnp.float32),
    )
    for head in range(H):
        start = head // 8 * 8
        values = jnp.concatenate(
            [sums[pl.ds(head, rows, stride=H), :], totals[start : start + 8]], axis=0
        )
        out_ref[(head % 2) ^ core, head // 2] = values.astype(jnp.bfloat16)


def attended_pieces(device, core, lengths, projected, cosine, sine, key_cache, value_cache):
    rows, slots = key_cache.shape[0], key_cache.shape[1]
    smem = pl.BlockSpec(memory_space=pltpu.SMEM)
    vmem = pl.BlockSpec(memory_space=pltpu.VMEM)
    return pl.pallas_call(
        attend_kernel,
        out_shape=jax.ShapeDtypeStruct((2, H // 2, rows + 8, HD), jnp.bfloat16),
        in_specs=[smem] * 2 + [vmem] * 4 + [pl.BlockSpec(memory_space=pltpu.HBM)] * 2,
        out_specs=vmem,
        scratch_shapes=[
            pltpu.VMEM(key_cache.shape, key_cache.dtype),
            pltpu.VMEM(value_cache.shape, value_cache.dtype),
            pltpu.SemaphoreType.DMA((rows // ROW_CHUNK,)),
            pltpu.SemaphoreType.DMA((rows // ROW_CHUNK,)),
            pltpu.VMEM((rows * H, HD), jnp.float32),
            pltpu.VMEM((rows * 2 * KVH, HD), jnp.float32),
            pltpu.VMEM((rows * H, HD), jnp.float32),
        ],
        compiler_params=pltpu.CompilerParams(vmem_limit_bytes=20 * 2**20),
        cost_estimate=pl.CostEstimate(
            flops=4 * rows * H * slots * HD,
            bytes_accessed=2 * (key_cache.size + value_cache.size),
            transcendentals=rows * H * slots,
        ),
    )(device, core, lengths, projected, cosine, sine, in_hbm(key_cache), in_hbm(value_cache))


def down_kernel(core_ref, rotated_ref, source_ref, out_ref, weights_ref, arrived):
    copies = column_copies(source_ref, weights_ref, arrived, DOWN_CHUNK)
    core = core_ref[0]
    rotated = rotated_ref[...]
    features = weights_ref.shape[1]
    width = out_ref.shape[3]
    block = max(width, min(256, features))
    for start in range(0, features, block):
        if start % DOWN_CHUNK == 0:
            copies[start // DOWN_CHUNK].wait()
        part = jnp.dot(
            rotated, weights_ref[:, start : start + block], preferred_element_type=jnp.float32
        ).astype(jnp.bfloat16)
        for offset in range(0, block, width):
            piece = (start + offset) // width
            out_ref[(piece % 2) ^ core, piece // 2] = part[:, offset : offset + width]


def down_pieces(core, rotated, w_down, devices):
    rows, features = rotated.shape[0], w_down.shape[1]
    vmem = pl.BlockSpec(memory_space=pltpu.VMEM)
    return pl.pallas_call(
        down_kernel,
        out_shape=jax.ShapeDtypeStruct((2, devices // 2, rows, features // devices), jnp.bfloat16),
        in_specs=[
            pl.BlockSpec(memory_space=pltpu.SMEM),
            vmem,
            pl.BlockSpec(memory_space=pltpu.HBM),
        ],
        out_specs=vmem,
        scratch_shapes=[
            pltpu.VMEM(w_down.shape, w_down.dtype),
            pltpu.SemaphoreType.DMA((w_down.shape[1] // DOWN_CHUNK,)),
        ],
        compiler_params=pltpu.CompilerParams(vmem_limit_bytes=12 * 2**20),
        cost_estimate=pl.CostEstimate(
            flops=2 * rows * rotated.shape[1] * features,
            bytes_accessed=w_down.size * 2,
            transcendentals=0,
        ),
    )(core, rotated, in_hbm(w_down))


def paley_table():
    prime = 13
    residues = [value * value % prime for value in range(1, prime)]
    conference = np.zeros((prime + 1, prime + 1))
    conference[0, 1:] = 1.0
    conference[1:, 0] = 1.0
    for row_number in range(prime):
        for col_number in range(prime):
            offset = (col_number - row_number) % prime
            if offset != 0:
                conference[row_number + 1, col_number + 1] = 1.0 if offset in residues else -1.0
    first_block = np.array([[1.0, -1.0], [-1.0, -1.0]])
    second_block = np.array([[1.0, 1.0], [1.0, -1.0]])
    return np.kron(conference, first_block) + np.kron(np.eye(prime + 1), second_block)


def sylvester_table(order):
    result = np.ones((1, 1))
    while result.shape[0] < order:
        result = np.kron(np.array([[1.0, 1.0], [1.0, -1.0]]), result)
    return result


def rotary_factors(positions):
    frequency = ROPE_BASE ** (-2.0 * jnp.arange(HD // 2, dtype=jnp.float32) / HD)
    angles = positions[:, None] * frequency[None, :]
    cosine, sine = jnp.cos(angles), jnp.sin(angles)
    return jnp.concatenate([cosine, cosine], axis=1), jnp.concatenate([-sine, sine], axis=1)


def per_device(hidden, w_qkv, key_cache, value_cache, lengths, w_out, w_gate, w_up, w_down):
    row_count = hidden.shape[0]
    devices = lax.axis_size("tensor")
    device_index = lax.axis_index("tensor")
    query_width = H * HD
    device = device_index.astype(jnp.int32).reshape(1)
    core = device % 2
    hidden_wide = hidden.astype(jnp.float32)
    blocks = H + 2 * KVH
    rows_used = (blocks + 1) * row_count
    rows_sent = -(-rows_used // (8 * devices)) * 8
    halves = projected_pieces(core, hidden, w_qkv, devices, rows_sent)
    halves, lengths = lax.optimization_barrier((halves, lengths))
    arrived = across(halves[1], 1)
    positions = lax.optimization_barrier(lengths.astype(jnp.float32))
    cosine, sine = rotary_factors(positions)
    lengths = jnp.broadcast_to(positions[:, None], (row_count, HD))
    arrived, cosine, sine, lengths = lax.optimization_barrier((arrived, cosine, sine, lengths))
    piece = scattered_joined(halves[0], arrived).astype(jnp.bfloat16)
    projected = gathered(piece)
    projected = projected.reshape(-1, HD)[:rows_used].reshape(blocks + 1, row_count, HD)
    direct = devices == H
    halves = attended_pieces(
        device, core if direct else jnp.zeros_like(core), lengths, projected, cosine, sine, key_cache, value_cache
    )
    if direct:
        parts = scattered_halves(halves[0], halves[1])
        parts, device_index = lax.optimization_barrier((parts, device_index))
        piece = normalized(device, parts, row_count)
    else:
        held = H * row_count // devices
        heads = halves.transpose(1, 0, 2, 3).reshape(H, row_count + 8, HD)
        numerators = heads[:, :row_count].reshape(devices, held, HD)
        totals = heads[:, row_count:].reshape(H // 8, 8, 8, HD)
        totals = jnp.einsum("ahhl->ahl", totals).reshape(H, HD)[:, :row_count]
        totals = jnp.pad(totals.reshape(devices, 1, held), ((0, 0), (0, 0), (0, HD - held)))
        parts = scattered_sum(jnp.concatenate([numerators, totals], axis=1))
        piece = (parts[:held] / parts[held, :held][:, None]).astype(jnp.bfloat16)
    attention = gathered_at_once(piece).reshape(H, row_count, HD).transpose(1, 0, 2).reshape(row_count, query_width)
    residual = (hidden_wide + jnp.dot(attention, w_out, preferred_element_type=jnp.float32)).astype(
        jnp.bfloat16
    )
    residual_full = gathered(residual).transpose(1, 0, 2).reshape(row_count, D)
    residual_wide = residual_full.astype(jnp.float32)
    normed = (
        residual_wide
        * lax.rsqrt(jnp.mean(residual_wide * residual_wide, axis=1, keepdims=True) + EPSILON)
    ).astype(jnp.bfloat16)
    gate = jnp.dot(normed, w_gate, preferred_element_type=jnp.float32)
    upward = jnp.dot(normed, w_up, preferred_element_type=jnp.float32)
    activation = jax.nn.silu(gate) * upward
    local_width = activation.shape[1]
    local_table = jnp.asarray(
        np.kron(sylvester_table(local_width // 28), paley_table()), dtype=jnp.float32
    )
    mixed = jnp.dot(activation, local_table, precision=lax.Precision.HIGH)
    rotated = (signed_sum(mixed) * FF ** (-0.5)).astype(jnp.bfloat16)
    halves = down_pieces(core, rotated, w_down, devices)
    down_share = scattered_halves(halves[0], halves[1])
    return (residual.astype(jnp.float32) + down_share).astype(jnp.bfloat16)


def solution(mesh):
    in_specs = (
        P("groups", "tensor"),
        P("tensor", None),
        P("groups", "tensor", None),
        P("groups", "tensor", None),
        P("groups"),
        P(None, "tensor"),
        P(None, "tensor"),
        P(None, "tensor"),
        P("tensor", None),
    )
    out_specs = P("groups", "tensor")
    return jax.shard_map(
        per_device, mesh=mesh, in_specs=in_specs, out_specs=out_specs, check_vma=False
    )
```

```python
import jax
import jax.numpy as jnp
import numpy as np
from jax import lax
from jax.experimental import pallas as pl
from jax.experimental.pallas import tpu as pltpu
from jax.sharding import PartitionSpec as P

D = 8192
FF = 14336
H = 32
KVH = 4
HD = 128


EPSILON = 1e-05
ROPE_BASE = 500000.0
QKV_CHUNK = 2560
DOWN_CHUNK = 1024
ROW_CHUNK = 8


def across(value, apart):
    pairs = [(source, source ^ apart) for source in range(lax.axis_size("tensor"))]
    return lax.ppermute(value, "tensor", pairs)


def same_core():
    devices = lax.axis_size("tensor")
    return [list(range(core, devices, 2)) for core in range(2)]


def scattered_sum(pieces):
    second = lax.axis_index("tensor") % 2 == 1
    halves = pieces.reshape(-1, 2, *pieces.shape[1:])
    kept = jnp.where(second, halves[:, 1], halves[:, 0])
    sent = jnp.where(second, halves[:, 0], halves[:, 1]).astype(jnp.bfloat16)
    return scattered_halves(kept, sent)


def scattered_halves(kept, sent):
    return scattered_joined(kept, across(sent, 1))


def scattered_joined(kept, arrived):
    joined = kept.astype(jnp.float32) + arrived.astype(jnp.float32)
    received = lax.all_to_all(
        joined.astype(jnp.bfloat16), "tensor", 0, 0, tiled=True, axis_index_groups=same_core()
    )
    return jnp.sum(received.astype(jnp.float32), axis=0)


def gathered_at_once(piece):
    copies = jnp.broadcast_to(piece[None], (lax.axis_size("tensor"), *piece.shape))
    return lax.all_to_all(copies, "tensor", 0, 0, tiled=True)


def gathered_same_core(piece):
    copies = jnp.broadcast_to(piece[None], (lax.axis_size("tensor") // 2, *piece.shape))
    return lax.all_to_all(copies, "tensor", 0, 0, tiled=True, axis_index_groups=same_core())


def gathered(piece):
    second = lax.axis_index("tensor") % 2 == 1
    mine = gathered_same_core(piece)
    theirs = across(mine, 1)
    both = jnp.stack([jnp.where(second, theirs, mine), jnp.where(second, mine, theirs)], axis=1)
    return both.reshape(-1, *piece.shape)


def signed_pair(value, apart):
    upper = lax.axis_index("tensor") // apart % 2 == 1
    partner = across(value, apart).astype(jnp.float32)
    own = value.astype(jnp.float32)
    return jnp.where(upper, partner - own, own + partner)


def signed_sum(value):
    devices = lax.axis_size("tensor")
    middle = devices // 4
    groups = [
        [top * devices // 2 + 2 * inner + core for inner in range(middle)]
        for top in range(2)
        for core in range(2)
    ]
    value = signed_pair(value, 1)
    value = signed_pair(value.astype(jnp.bfloat16), devices // 2).astype(jnp.bfloat16)
    copies = jnp.broadcast_to(value[None], (middle, *value.shape))
    received = lax.all_to_all(copies, "tensor", 0, 0, tiled=True, axis_index_groups=groups)
    received, index = lax.optimization_barrier((received, lax.axis_index("tensor")))
    common = jnp.arange(middle) & (index // 2 % middle)
    for shift in (4, 2, 1):
        common = common ^ (common >> shift)
    signs = 1.0 - 2.0 * (common & 1).astype(jnp.float32)
    return jnp.sum(received.astype(jnp.float32) * signs[:, None, None], axis=0)


def normalize_kernel(device_ref, parts_ref, out_ref):
    rows = out_ref.shape[0]
    shape = (8, HD)
    chosen = lax.broadcasted_iota(jnp.int32, shape, 0) == device_ref[0] // 2 % 8
    totals = jnp.sum(jnp.where(chosen, parts_ref[rows : rows + 8], 0.0), axis=0, keepdims=True)
    shape = (rows, HD)
    own = lax.broadcasted_iota(jnp.int32, shape, 0) == lax.broadcasted_iota(jnp.int32, shape, 1)
    column = jnp.sum(jnp.where(own, totals, 0.0), axis=1, keepdims=True)
    out_ref[...] = (parts_ref[:rows] / column).astype(jnp.bfloat16)


def normalized(device, parts, rows):
    vmem = pl.BlockSpec(memory_space=pltpu.VMEM)
    return pl.pallas_call(
        normalize_kernel,
        out_shape=jax.ShapeDtypeStruct((rows, HD), jnp.bfloat16),
        in_specs=[pl.BlockSpec(memory_space=pltpu.SMEM), vmem],
        out_specs=vmem,
        compiler_params=pltpu.CompilerParams(vmem_limit_bytes=2**20),
        cost_estimate=pl.CostEstimate(flops=10000, bytes_accessed=10000, transcendentals=0),
    )(device, parts)


def in_hbm(value):
    return pltpu.with_memory_space_constraint(value, pltpu.HBM)


def column_copies(weights_ref, held_ref, arrived, chunk):
    copies = []
    for start in range(0, weights_ref.shape[1], chunk):
        part = (slice(None), pl.ds(start, chunk))
        copies.append(
            pltpu.make_async_copy(
                weights_ref.at[part], held_ref.at[part], arrived.at[start // chunk]
            )
        )
        copies[-1].start()
    return copies


def project_kernel(
    core_ref, hidden_source, source_ref, out_ref, hidden_ref, hidden_arrived, weights_ref, arrived, stacked
):
    hidden_copy = pltpu.make_async_copy(hidden_source, hidden_ref, hidden_arrived)
    hidden_copy.start()
    copies = column_copies(source_ref, weights_ref, arrived, QKV_CHUNK)
    core = core_ref[0]
    rows = hidden_ref.shape[0]
    columns = weights_ref.shape[1]
    hidden_copy.wait()
    hidden = hidden_ref[...]
    wide = hidden.astype(jnp.float32)
    squares = jnp.sum(wide * wide, axis=1, keepdims=True)
    half = stacked.shape[0] // 2
    heads = H // 2
    fresh = KVH // 2

    def place(block):
        if block < H:
            return block // heads * half + block % heads * rows
        block -= H
        kind, head = block // KVH, block % KVH
        return head // fresh * half + (heads + kind * fresh + head % fresh) * rows

    for start in range(0, columns, 2 * HD):
        if start % QKV_CHUNK == 0:
            copies[start // QKV_CHUNK].wait()
        part = jnp.dot(
            hidden, weights_ref[:, start : start + 2 * HD], preferred_element_type=jnp.float32
        )
        for offset in range(2):
            first = place(start // HD + offset)
            stacked[first : first + rows] = part[:, offset * HD : (offset + 1) * HD]
    held = out_ref.shape[2]
    for pair in range(2):
        used = pair * half + (heads + 2 * fresh) * rows
        stacked[used : used + rows] = jnp.broadcast_to(squares, (rows, HD))
        left = (pair + 1) * half - used - rows
        if left:
            stacked[used + rows : used + rows + left] = jnp.zeros((left, HD), jnp.float32)
        for piece in range(half // held):
            first = pair * half + piece * held
            values = stacked[first : first + held].astype(jnp.bfloat16)
            out_ref[pair ^ core ^ 1, piece] = values


def projected_pieces(core, hidden, w_qkv, devices, rows_sent):
    vmem = pl.BlockSpec(memory_space=pltpu.VMEM)
    return pl.pallas_call(
        project_kernel,
        out_shape=jax.ShapeDtypeStruct((2, devices // 2, rows_sent, HD), jnp.bfloat16),
        in_specs=[
            pl.BlockSpec(memory_space=pltpu.SMEM),
            pl.BlockSpec(memory_space=pltpu.HBM),
            pl.BlockSpec(memory_space=pltpu.HBM),
        ],
        out_specs=vmem,
        scratch_shapes=[
            pltpu.VMEM(hidden.shape, hidden.dtype),
            pltpu.SemaphoreType.DMA,
            pltpu.VMEM(w_qkv.shape, w_qkv.dtype),
            pltpu.SemaphoreType.DMA((w_qkv.shape[1] // QKV_CHUNK,)),
            pltpu.VMEM((devices * rows_sent, HD), jnp.float32),
        ],
        compiler_params=pltpu.CompilerParams(vmem_limit_bytes=8 * 2**20),
        cost_estimate=pl.CostEstimate(
            flops=2 * hidden.shape[0] * w_qkv.size, bytes_accessed=2 * w_qkv.size, transcendentals=0
        ),
    )(core, in_hbm(hidden), in_hbm(w_qkv))


def attend_kernel(
    device_ref, pair_ref, lengths_ref, projected_ref, cosine_ref, sine_ref, key_source, value_source,
    out_ref, keys_ref, values_ref, keys_arrived, values_arrived, queries, fresh, sums,
):
    rows, slots, width = keys_ref.shape
    columns = pl.ds(pl.multiple_of(pair_ref[0] * width, width), width)

    def copies(index):
        part = pl.ds(index * ROW_CHUNK, ROW_CHUNK)
        return (
            pltpu.make_async_copy(
                key_source.at[part, :, columns], keys_ref.at[part], keys_arrived.at[index]
            ),
            pltpu.make_async_copy(
                value_source.at[part, :, columns], values_ref.at[part], values_arrived.at[index]
            ),
        )

    for index in range(rows // ROW_CHUNK):
        for copy in copies(index):
            copy.start()
    device = device_ref[0]
    group = H // KVH
    heads = 2 * group
    scale = HD ** (-0.5)
    cosine, sine = cosine_ref[...], sine_ref[...]
    inverse = lax.rsqrt(projected_ref[heads + 4].astype(jnp.float32) / D + EPSILON)

    def block(index):
        value = projected_ref[index].astype(jnp.float32) * inverse
        return value.astype(jnp.bfloat16).astype(jnp.float32)

    def turned(index):
        value = block(index)
        value = value * cosine + pltpu.roll(value, HD // 2, 1) * sine
        return value.astype(jnp.bfloat16).astype(jnp.float32)

    for head in range(heads):
        queries[pl.ds(head, rows, stride=heads), :] = turned(head)
    for head in range(2):
        fresh[pl.ds(head, rows, stride=4), :] = turned(heads + head)
        fresh[pl.ds(2 + head, rows, stride=4), :] = block(heads + 2 + head)

    lane = lax.broadcasted_iota(jnp.int32, (1, slots), 1) + device * slots
    lane = lane.astype(jnp.float32)
    row_lane = lax.broadcasted_iota(jnp.int32, (heads, HD), 1)
    lower = lax.broadcasted_iota(jnp.int32, (heads, HD), 0) < group

    def expand(first):
        picked = [jnp.broadcast_to(fresh[pl.ds(first + head, 1), :], (group, HD)) for head in range(2)]
        return jnp.concatenate(picked, axis=0)

    def some_rows(step, totals):
        numbers = [step * ROW_CHUNK + offset for offset in range(ROW_CHUNK)]
        scores = []
        own = []
        copies(step)[0].wait()
        for row in numbers:
            query = queries[pl.ds(pl.multiple_of(row * heads, heads), heads), :]
            own_score = jnp.sum(query * expand(row * 4), axis=1, keepdims=True) * scale
            own.append(jnp.where(device == 0, jnp.exp(own_score), 0.0))
            spread = jnp.concatenate(
                [jnp.where(lower, query, 0.0), jnp.where(lower, 0.0, query)], axis=1
            ).astype(jnp.bfloat16)
            scores.append(
                lax.dot_general(
                    spread,
                    keys_ref[row],
                    (((1,), (1,)), ((), ())),
                    preferred_element_type=jnp.float32,
                )
            )
        weights = [
            jnp.where(lane < lengths_ref[pl.ds(row, 1), :1], jnp.exp(score * scale), 0.0)
            for row, score in zip(numbers, scores)
        ]
        copies(step)[1].wait()
        for row, weight, own_weight in zip(numbers, weights, own):
            product = jnp.dot(
                weight.astype(jnp.bfloat16), values_ref[row], preferred_element_type=jnp.float32
            )
            chosen = jnp.concatenate([product[:group, :HD], product[group:, HD:]], axis=0)
            total = jnp.sum(weight, axis=1, keepdims=True) + own_weight
            summed = chosen + own_weight * expand(row * 4 + 2)
            sums[pl.ds(pl.multiple_of(row * heads, heads), heads), :] = summed
            totals = jnp.where(row_lane == row, total, totals)
        return totals

    totals = lax.fori_loop(
        0, rows // ROW_CHUNK, some_rows, jnp.zeros((heads, HD), jnp.float32)
    )
    for head in range(heads):
        start = head // 8 * 8
        values = jnp.concatenate(
            [sums[pl.ds(head, rows, stride=heads), :], totals[start : start + 8]], axis=0
        )
        out_ref[head] = values.astype(jnp.bfloat16)


def attended_pair(device, pair, lengths, projected, cosine, sine, key_cache, value_cache):
    rows, slots = key_cache.shape[0], key_cache.shape[1]
    smem = pl.BlockSpec(memory_space=pltpu.SMEM)
    vmem = pl.BlockSpec(memory_space=pltpu.VMEM)
    projected = projected.reshape(-1, HD)[: (H // 2 + 5) * rows].reshape(H // 2 + 5, rows, HD)
    return pl.pallas_call(
        attend_kernel,
        out_shape=jax.ShapeDtypeStruct((H // 2, rows + 8, HD), jnp.bfloat16),
        in_specs=[smem] * 2 + [vmem] * 4 + [pl.BlockSpec(memory_space=pltpu.HBM)] * 2,
        out_specs=vmem,
        scratch_shapes=[
            pltpu.VMEM((rows, slots, 2 * HD), key_cache.dtype),
            pltpu.VMEM((rows, slots, 2 * HD), value_cache.dtype),
            pltpu.SemaphoreType.DMA((rows // ROW_CHUNK,)),
            pltpu.SemaphoreType.DMA((rows // ROW_CHUNK,)),
            pltpu.VMEM((rows * H // 2, HD), jnp.float32),
            pltpu.VMEM((rows * 4, HD), jnp.float32),
            pltpu.VMEM((rows * H // 2, HD), jnp.float32),
        ],
        compiler_params=pltpu.CompilerParams(vmem_limit_bytes=12 * 2**20),
        cost_estimate=pl.CostEstimate(
            flops=2 * rows * H * slots * HD,
            bytes_accessed=key_cache.size + value_cache.size,
            transcendentals=rows * H * slots // 2,
        ),
    )(device, pair, lengths, projected, cosine, sine, in_hbm(key_cache), in_hbm(value_cache))


def down_kernel(core_ref, rotated_ref, source_ref, out_ref, weights_ref, arrived):
    copies = column_copies(source_ref, weights_ref, arrived, DOWN_CHUNK)
    core = core_ref[0]
    rotated = rotated_ref[...]
    features = weights_ref.shape[1]
    width = out_ref.shape[3]
    block = max(width, min(256, features))
    for start in range(0, features, block):
        if start % DOWN_CHUNK == 0:
            copies[start // DOWN_CHUNK].wait()
        part = jnp.dot(
            rotated, weights_ref[:, start : start + block], preferred_element_type=jnp.float32
        ).astype(jnp.bfloat16)
        for offset in range(0, block, width):
            piece = (start + offset) // width
            out_ref[(piece % 2) ^ core, piece // 2] = part[:, offset : offset + width]


def down_pieces(core, rotated, w_down, devices):
    rows, features = rotated.shape[0], w_down.shape[1]
    vmem = pl.BlockSpec(memory_space=pltpu.VMEM)
    return pl.pallas_call(
        down_kernel,
        out_shape=jax.ShapeDtypeStruct((2, devices // 2, rows, features // devices), jnp.bfloat16),
        in_specs=[
            pl.BlockSpec(memory_space=pltpu.SMEM),
            vmem,
            pl.BlockSpec(memory_space=pltpu.HBM),
        ],
        out_specs=vmem,
        scratch_shapes=[
            pltpu.VMEM(w_down.shape, w_down.dtype),
            pltpu.SemaphoreType.DMA((w_down.shape[1] // DOWN_CHUNK,)),
        ],
        compiler_params=pltpu.CompilerParams(vmem_limit_bytes=12 * 2**20),
        cost_estimate=pl.CostEstimate(
            flops=2 * rows * rotated.shape[1] * features,
            bytes_accessed=w_down.size * 2,
            transcendentals=0,
        ),
    )(core, rotated, in_hbm(w_down))


def paley_table():
    prime = 13
    residues = [value * value % prime for value in range(1, prime)]
    conference = np.zeros((prime + 1, prime + 1))
    conference[0, 1:] = 1.0
    conference[1:, 0] = 1.0
    for row_number in range(prime):
        for col_number in range(prime):
            offset = (col_number - row_number) % prime
            if offset != 0:
                conference[row_number + 1, col_number + 1] = 1.0 if offset in residues else -1.0
    first_block = np.array([[1.0, -1.0], [-1.0, -1.0]])
    second_block = np.array([[1.0, 1.0], [1.0, -1.0]])
    return np.kron(conference, first_block) + np.kron(np.eye(prime + 1), second_block)


def sylvester_table(order):
    result = np.ones((1, 1))
    while result.shape[0] < order:
        result = np.kron(np.array([[1.0, 1.0], [1.0, -1.0]]), result)
    return result


def rotary_factors(positions):
    frequency = ROPE_BASE ** (-2.0 * jnp.arange(HD // 2, dtype=jnp.float32) / HD)
    angles = positions[:, None] * frequency[None, :]
    cosine, sine = jnp.cos(angles), jnp.sin(angles)
    return jnp.concatenate([cosine, cosine], axis=1), jnp.concatenate([-sine, sine], axis=1)


def per_device(hidden, w_qkv, key_cache, value_cache, lengths, w_out, w_gate, w_up, w_down):
    row_count = hidden.shape[0]
    devices = lax.axis_size("tensor")
    device_index = lax.axis_index("tensor")
    query_width = H * HD
    device = device_index.astype(jnp.int32).reshape(1)
    core = device % 2
    hidden_wide = hidden.astype(jnp.float32)
    rows_used = (H // 2 + KVH + 1) * row_count
    rows_sent = -(-rows_used // (4 * devices)) * 8
    halves = projected_pieces(core, hidden, w_qkv, devices, rows_sent)
    halves, lengths = lax.optimization_barrier((halves, lengths))
    arrived = across(halves[1], 1)
    positions = lax.optimization_barrier(lengths.astype(jnp.float32))
    cosine, sine = rotary_factors(positions)
    lengths = jnp.broadcast_to(positions[:, None], (row_count, HD))
    arrived, cosine, sine, lengths, other = lax.optimization_barrier(
        (arrived, cosine, sine, lengths, 1 - core)
    )
    piece = scattered_joined(halves[0], arrived).astype(jnp.bfloat16)
    mine = gathered_same_core(piece)
    theirs = across(mine, 1)
    second = device_index % 2 == 1
    both = lax.optimization_barrier((jnp.where(second, mine, theirs), jnp.where(second, theirs, mine)))
    theirs = jnp.where(second, both[1], both[0])
    shared = (lengths, cosine, sine, key_cache, value_cache)
    attend = lambda pair, projected: attended_pair(
        device, pair, shared[0], projected, shared[1], shared[2], shared[3], shared[4]
    )
    sent = attend(other, mine)
    arrived = across(sent, 1)
    kept = attend(core, theirs)
    if devices == H:
        parts = scattered_joined(kept, arrived)
        parts, device_index = lax.optimization_barrier((parts, device_index))
        piece = normalized(device, parts, row_count)
        heads = gathered_at_once(piece).reshape(devices // 2, 2, row_count, HD)
        attention = heads.transpose(2, 1, 0, 3).reshape(row_count, query_width)
    else:
        held = H * row_count // devices
        first = core[0] == 0
        heads = jnp.concatenate([jnp.where(first, kept, sent), jnp.where(first, sent, kept)])
        numerators = heads[:, :row_count].reshape(devices, held, HD)
        totals = heads[:, row_count:].reshape(H // 8, 8, 8, HD)
        totals = jnp.einsum("ahhl->ahl", totals).reshape(H, HD)[:, :row_count]
        totals = jnp.pad(totals.reshape(devices, 1, held), ((0, 0), (0, 0), (0, HD - held)))
        parts = scattered_sum(jnp.concatenate([numerators, totals], axis=1))
        piece = (parts[:held] / parts[held, :held][:, None]).astype(jnp.bfloat16)
        heads = gathered_at_once(piece).reshape(H, row_count, HD)
        attention = heads.transpose(1, 0, 2).reshape(row_count, query_width)
    residual = (hidden_wide + jnp.dot(attention, w_out, preferred_element_type=jnp.float32)).astype(
        jnp.bfloat16
    )
    residual_full = gathered(residual).transpose(1, 0, 2).reshape(row_count, D)
    residual_wide = residual_full.astype(jnp.float32)
    normed = (
        residual_wide
        * lax.rsqrt(jnp.mean(residual_wide * residual_wide, axis=1, keepdims=True) + EPSILON)
    ).astype(jnp.bfloat16)
    gate = jnp.dot(normed, w_gate, preferred_element_type=jnp.float32)
    upward = jnp.dot(normed, w_up, preferred_element_type=jnp.float32)
    activation = jax.nn.silu(gate) * upward
    local_width = activation.shape[1]
    local_table = jnp.asarray(
        np.kron(sylvester_table(local_width // 28), paley_table()), dtype=jnp.float32
    )
    mixed = jnp.dot(activation, local_table, precision=lax.Precision.HIGH)
    rotated = (signed_sum(mixed) * FF ** (-0.5)).astype(jnp.bfloat16)
    halves = down_pieces(core, rotated, w_down, devices)
    down_share = scattered_halves(halves[0], halves[1])
    return (residual.astype(jnp.float32) + down_share).astype(jnp.bfloat16)


def solution(mesh):
    in_specs = (
        P("groups", "tensor"),
        P("tensor", None),
        P("groups", "tensor", None),
        P("groups", "tensor", None),
        P("groups"),
        P(None, "tensor"),
        P(None, "tensor"),
        P(None, "tensor"),
        P("tensor", None),
    )
    out_specs = P("groups", "tensor")
    return jax.shard_map(
        per_device, mesh=mesh, in_specs=in_specs, out_specs=out_specs, check_vma=False
    )
```

```python
import jax
import jax.numpy as jnp
import numpy as np
from jax import lax
from jax.experimental import pallas as pl
from jax.experimental.pallas import tpu as pltpu
from jax.sharding import PartitionSpec as P

D = 8192
FF = 14336
H = 32
KVH = 4
HD = 128


EPSILON = 1e-05
ROPE_BASE = 500000.0
QKV_CHUNK = 2560
ROW_CHUNK = 8


def across(value, apart):
    pairs = [(source, source ^ apart) for source in range(lax.axis_size("tensor"))]
    return lax.ppermute(value, "tensor", pairs)


def same_core():
    devices = lax.axis_size("tensor")
    return [list(range(core, devices, 2)) for core in range(2)]


def scattered_sum(pieces, second):
    halves = pieces.reshape(-1, 2, *pieces.shape[1:])
    kept = jnp.where(second, halves[:, 1], halves[:, 0])
    sent = jnp.where(second, halves[:, 0], halves[:, 1]).astype(jnp.bfloat16)
    return scattered_halves(kept, sent)


def scattered_halves(kept, sent):
    return scattered_joined(kept, across(sent, 1))


def scattered_joined(kept, arrived):
    joined = kept.astype(jnp.float32) + arrived.astype(jnp.float32)
    received = lax.all_to_all(
        joined.astype(jnp.bfloat16), "tensor", 0, 0, tiled=True, axis_index_groups=same_core()
    )
    return jnp.sum(received.astype(jnp.float32), axis=0)


def gathered_at_once(piece):
    copies = jnp.broadcast_to(piece[None], (lax.axis_size("tensor"), *piece.shape))
    return lax.all_to_all(copies, "tensor", 0, 0, tiled=True)


def gathered_same_core(piece):
    copies = jnp.broadcast_to(piece[None], (lax.axis_size("tensor") // 2, *piece.shape))
    return lax.all_to_all(copies, "tensor", 0, 0, tiled=True, axis_index_groups=same_core())


def gathered(piece, second):
    mine = gathered_same_core(piece)
    theirs = across(mine, 1)
    both = jnp.stack([jnp.where(second, theirs, mine), jnp.where(second, mine, theirs)], axis=1)
    return both.reshape(-1, *piece.shape)


def signed_join(value, partner, upper):
    own, partner = value.astype(jnp.float32), partner.astype(jnp.float32)
    return jnp.where(upper, partner - own, own + partner)


def middle_signs(index, middle):
    common = jnp.arange(middle) & (index // 2 % middle)
    for shift in (4, 2, 1):
        common = common ^ (common >> shift)
    return 1.0 - 2.0 * (common & 1).astype(jnp.float32)


def signed_sum(value, second, upper, signs):
    devices = lax.axis_size("tensor")
    middle = devices // 4
    groups = [
        [top * devices // 2 + 2 * inner + core for inner in range(middle)]
        for top in range(2)
        for core in range(2)
    ]
    value = signed_join(value, across(value, 1), second)
    value = value.astype(jnp.bfloat16)
    value = signed_join(value, across(value, devices // 2), upper).astype(jnp.bfloat16)
    copies = jnp.broadcast_to(value[None], (middle, *value.shape))
    received = lax.all_to_all(copies, "tensor", 0, 0, tiled=True, axis_index_groups=groups)
    return jnp.sum(received.astype(jnp.float32) * signs[:, None, None], axis=0)


def normalize_kernel(device_ref, parts_ref, out_ref):
    rows = out_ref.shape[0]
    shape = (8, HD)
    chosen = lax.broadcasted_iota(jnp.int32, shape, 0) == device_ref[0] // 2 % 8
    totals = jnp.sum(jnp.where(chosen, parts_ref[rows : rows + 8], 0.0), axis=0, keepdims=True)
    shape = (rows, HD)
    own = lax.broadcasted_iota(jnp.int32, shape, 0) == lax.broadcasted_iota(jnp.int32, shape, 1)
    column = jnp.sum(jnp.where(own, totals, 0.0), axis=1, keepdims=True)
    out_ref[...] = (parts_ref[:rows] / column).astype(jnp.bfloat16)


def normalized(device, parts, rows):
    vmem = pl.BlockSpec(memory_space=pltpu.VMEM)
    return pl.pallas_call(
        normalize_kernel,
        out_shape=jax.ShapeDtypeStruct((rows, HD), jnp.bfloat16),
        in_specs=[pl.BlockSpec(memory_space=pltpu.SMEM), vmem],
        out_specs=vmem,
        compiler_params=pltpu.CompilerParams(vmem_limit_bytes=2**20),
        cost_estimate=pl.CostEstimate(flops=10000, bytes_accessed=10000, transcendentals=0),
    )(device, parts)


def in_hbm(value):
    return pltpu.with_memory_space_constraint(value, pltpu.HBM)


def column_copies(weights_ref, held_ref, arrived, chunk):
    copies = []
    for start in range(0, weights_ref.shape[1], chunk):
        part = (slice(None), pl.ds(start, chunk))
        copies.append(
            pltpu.make_async_copy(
                weights_ref.at[part], held_ref.at[part], arrived.at[start // chunk]
            )
        )
        copies[-1].start()
    return copies


def project_kernel(
    core_ref, hidden_source, source_ref, out_ref, hidden_ref, hidden_arrived, weights_ref, arrived, stacked
):
    hidden_copy = pltpu.make_async_copy(hidden_source, hidden_ref, hidden_arrived)
    hidden_copy.start()
    copies = column_copies(source_ref, weights_ref, arrived, QKV_CHUNK)
    core = core_ref[0]
    rows = hidden_ref.shape[0]
    columns = weights_ref.shape[1]
    hidden_copy.wait()
    hidden = hidden_ref[...]
    wide = hidden.astype(jnp.float32)
    squares = jnp.sum(wide * wide, axis=1, keepdims=True)
    half = stacked.shape[0] // 2
    heads = H // 2
    fresh = KVH // 2

    def place(block):
        if block < H:
            return block // heads * half + block % heads * rows
        block -= H
        kind, head = block // KVH, block % KVH
        return head // fresh * half + (heads + kind * fresh + head % fresh) * rows

    for start in range(0, columns, 2 * HD):
        if start % QKV_CHUNK == 0:
            copies[start // QKV_CHUNK].wait()
        part = jnp.dot(
            hidden, weights_ref[:, start : start + 2 * HD], preferred_element_type=jnp.float32
        )
        for offset in range(2):
            first = place(start // HD + offset)
            stacked[first : first + rows] = part[:, offset * HD : (offset + 1) * HD]
    held = out_ref.shape[2]
    for pair in range(2):
        used = pair * half + (heads + 2 * fresh) * rows
        stacked[used : used + rows] = jnp.broadcast_to(squares, (rows, HD))
        left = (pair + 1) * half - used - rows
        if left:
            stacked[used + rows : used + rows + left] = jnp.zeros((left, HD), jnp.float32)
        for piece in range(half // held):
            first = pair * half + piece * held
            values = stacked[first : first + held].astype(jnp.bfloat16)
            out_ref[pair ^ core ^ 1, piece] = values


def projected_pieces(core, hidden, w_qkv, devices, rows_sent):
    vmem = pl.BlockSpec(memory_space=pltpu.VMEM)
    return pl.pallas_call(
        project_kernel,
        out_shape=jax.ShapeDtypeStruct((2, devices // 2, rows_sent, HD), jnp.bfloat16),
        in_specs=[
            pl.BlockSpec(memory_space=pltpu.SMEM),
            pl.BlockSpec(memory_space=pltpu.HBM),
            pl.BlockSpec(memory_space=pltpu.HBM),
        ],
        out_specs=vmem,
        scratch_shapes=[
            pltpu.VMEM(hidden.shape, hidden.dtype),
            pltpu.SemaphoreType.DMA,
            pltpu.VMEM(w_qkv.shape, w_qkv.dtype),
            pltpu.SemaphoreType.DMA((w_qkv.shape[1] // QKV_CHUNK,)),
            pltpu.VMEM((devices * rows_sent, HD), jnp.float32),
        ],
        compiler_params=pltpu.CompilerParams(vmem_limit_bytes=8 * 2**20),
        cost_estimate=pl.CostEstimate(
            flops=2 * hidden.shape[0] * w_qkv.size, bytes_accessed=2 * w_qkv.size, transcendentals=0
        ),
    )(core, in_hbm(hidden), in_hbm(w_qkv))


def attend_kernel(
    device_ref, pair_ref, lengths_ref, projected_ref, cosine_ref, sine_ref, key_source, value_source,
    out_ref, keys_ref, values_ref, keys_arrived, values_arrived, queries, fresh, sums,
):
    rows, slots, width = keys_ref.shape
    columns = pl.ds(pl.multiple_of(pair_ref[0] * width, width), width)

    def copies(index):
        part = pl.ds(index * ROW_CHUNK, ROW_CHUNK)
        return (
            pltpu.make_async_copy(
                key_source.at[part, :, columns], keys_ref.at[part], keys_arrived.at[index]
            ),
            pltpu.make_async_copy(
                value_source.at[part, :, columns], values_ref.at[part], values_arrived.at[index]
            ),
        )

    for index in range(rows // ROW_CHUNK):
        for copy in copies(index):
            copy.start()
    device = device_ref[0]
    group = H // KVH
    heads = 2 * group
    scale = HD ** (-0.5)
    cosine, sine = cosine_ref[...], sine_ref[...]
    inverse = lax.rsqrt(projected_ref[heads + 4].astype(jnp.float32) / D + EPSILON)

    def block(index):
        value = projected_ref[index].astype(jnp.float32) * inverse
        return value.astype(jnp.bfloat16).astype(jnp.float32)

    def turned(index):
        value = block(index)
        value = value * cosine + pltpu.roll(value, HD // 2, 1) * sine
        return value.astype(jnp.bfloat16).astype(jnp.float32)

    for head in range(heads):
        queries[pl.ds(head, rows, stride=heads), :] = turned(head)
    for head in range(2):
        fresh[pl.ds(head, rows, stride=4), :] = turned(heads + head)
        fresh[pl.ds(2 + head, rows, stride=4), :] = block(heads + 2 + head)

    lane = lax.broadcasted_iota(jnp.int32, (1, slots), 1) + device * slots
    lane = lane.astype(jnp.float32)
    row_lane = lax.broadcasted_iota(jnp.int32, (heads, HD), 1)
    lower = lax.broadcasted_iota(jnp.int32, (heads, HD), 0) < group

    def expand(first):
        picked = [jnp.broadcast_to(fresh[pl.ds(first + head, 1), :], (group, HD)) for head in range(2)]
        return jnp.concatenate(picked, axis=0)

    def some_rows(step, totals):
        numbers = [step * ROW_CHUNK + offset for offset in range(ROW_CHUNK)]
        scores = []
        own = []
        copies(step)[0].wait()
        for row in numbers:
            query = queries[pl.ds(pl.multiple_of(row * heads, heads), heads), :]
            own_score = jnp.sum(query * expand(row * 4), axis=1, keepdims=True) * scale
            own.append(jnp.where(device == 0, jnp.exp(own_score), 0.0))
            spread = jnp.concatenate(
                [jnp.where(lower, query, 0.0), jnp.where(lower, 0.0, query)], axis=1
            ).astype(jnp.bfloat16)
            scores.append(
                lax.dot_general(
                    spread,
                    keys_ref[row],
                    (((1,), (1,)), ((), ())),
                    preferred_element_type=jnp.float32,
                )
            )
        weights = [
            jnp.where(lane < lengths_ref[pl.ds(row, 1), :1], jnp.exp(score * scale), 0.0)
            for row, score in zip(numbers, scores)
        ]
        copies(step)[1].wait()
        for row, weight, own_weight in zip(numbers, weights, own):
            product = jnp.dot(
                weight.astype(jnp.bfloat16), values_ref[row], preferred_element_type=jnp.float32
            )
            chosen = jnp.concatenate([product[:group, :HD], product[group:, HD:]], axis=0)
            total = jnp.sum(weight, axis=1, keepdims=True) + own_weight
            summed = chosen + own_weight * expand(row * 4 + 2)
            sums[pl.ds(pl.multiple_of(row * heads, heads), heads), :] = summed
            totals = jnp.where(row_lane == row, total, totals)
        return totals

    totals = lax.fori_loop(
        0, rows // ROW_CHUNK, some_rows, jnp.zeros((heads, HD), jnp.float32)
    )
    for head in range(heads):
        start = head // 8 * 8
        values = jnp.concatenate(
            [sums[pl.ds(head, rows, stride=heads), :], totals[start : start + 8]], axis=0
        )
        out_ref[head] = values.astype(jnp.bfloat16)


def attended_pair(device, pair, lengths, projected, cosine, sine, key_cache, value_cache):
    rows, slots = key_cache.shape[0], key_cache.shape[1]
    smem = pl.BlockSpec(memory_space=pltpu.SMEM)
    vmem = pl.BlockSpec(memory_space=pltpu.VMEM)
    projected = projected.reshape(-1, HD)[: (H // 2 + 5) * rows].reshape(H // 2 + 5, rows, HD)
    return pl.pallas_call(
        attend_kernel,
        out_shape=jax.ShapeDtypeStruct((H // 2, rows + 8, HD), jnp.bfloat16),
        in_specs=[smem] * 2 + [vmem] * 4 + [pl.BlockSpec(memory_space=pltpu.HBM)] * 2,
        out_specs=vmem,
        scratch_shapes=[
            pltpu.VMEM((rows, slots, 2 * HD), key_cache.dtype),
            pltpu.VMEM((rows, slots, 2 * HD), value_cache.dtype),
            pltpu.SemaphoreType.DMA((rows // ROW_CHUNK,)),
            pltpu.SemaphoreType.DMA((rows // ROW_CHUNK,)),
            pltpu.VMEM((rows * H // 2, HD), jnp.float32),
            pltpu.VMEM((rows * 4, HD), jnp.float32),
            pltpu.VMEM((rows * H // 2, HD), jnp.float32),
        ],
        compiler_params=pltpu.CompilerParams(vmem_limit_bytes=12 * 2**20),
        cost_estimate=pl.CostEstimate(
            flops=2 * rows * H * slots * HD,
            bytes_accessed=key_cache.size + value_cache.size,
            transcendentals=rows * H * slots // 2,
        ),
    )(device, pair, lengths, projected, cosine, sine, in_hbm(key_cache), in_hbm(value_cache))


def down_kernel(core_ref, rotated_ref, weights_ref, out_ref):
    core = core_ref[0]
    rotated = rotated_ref[...]
    features = weights_ref.shape[1]
    width = out_ref.shape[3]
    block = max(width, min(256, features))
    for start in range(0, features, block):
        part = jnp.dot(
            rotated, weights_ref[:, start : start + block], preferred_element_type=jnp.float32
        ).astype(jnp.bfloat16)
        for offset in range(0, block, width):
            piece = (start + offset) // width
            out_ref[(piece % 2) ^ core, piece // 2] = part[:, offset : offset + width]


def down_pieces(core, rotated, w_down, devices):
    rows, features = rotated.shape[0], w_down.shape[1]
    vmem = pl.BlockSpec(memory_space=pltpu.VMEM)
    return pl.pallas_call(
        down_kernel,
        out_shape=jax.ShapeDtypeStruct((2, devices // 2, rows, features // devices), jnp.bfloat16),
        in_specs=[pl.BlockSpec(memory_space=pltpu.SMEM), vmem, vmem],
        out_specs=vmem,
        compiler_params=pltpu.CompilerParams(vmem_limit_bytes=12 * 2**20),
        cost_estimate=pl.CostEstimate(
            flops=2 * rows * rotated.shape[1] * features,
            bytes_accessed=w_down.size * 2,
            transcendentals=0,
        ),
    )(core, rotated, w_down)


def paley_table():
    prime = 13
    residues = [value * value % prime for value in range(1, prime)]
    conference = np.zeros((prime + 1, prime + 1))
    conference[0, 1:] = 1.0
    conference[1:, 0] = 1.0
    for row_number in range(prime):
        for col_number in range(prime):
            offset = (col_number - row_number) % prime
            if offset != 0:
                conference[row_number + 1, col_number + 1] = 1.0 if offset in residues else -1.0
    first_block = np.array([[1.0, -1.0], [-1.0, -1.0]])
    second_block = np.array([[1.0, 1.0], [1.0, -1.0]])
    return np.kron(conference, first_block) + np.kron(np.eye(prime + 1), second_block)


def sylvester_table(order):
    result = np.ones((1, 1))
    while result.shape[0] < order:
        result = np.kron(np.array([[1.0, 1.0], [1.0, -1.0]]), result)
    return result


def rotary_factors(positions):
    frequency = ROPE_BASE ** (-2.0 * jnp.arange(HD // 2, dtype=jnp.float32) / HD)
    angles = positions[:, None] * frequency[None, :]
    cosine, sine = jnp.cos(angles), jnp.sin(angles)
    return jnp.concatenate([cosine, cosine], axis=1), jnp.concatenate([-sine, sine], axis=1)


def per_device(hidden, w_qkv, key_cache, value_cache, lengths, w_out, w_gate, w_up, w_down):
    row_count = hidden.shape[0]
    devices = lax.axis_size("tensor")
    device_index = lax.axis_index("tensor")
    query_width = H * HD
    device = device_index.astype(jnp.int32).reshape(1)
    core = device % 2
    hidden_wide = hidden.astype(jnp.float32)
    rows_used = (H // 2 + KVH + 1) * row_count
    rows_sent = -(-rows_used // (4 * devices)) * 8
    halves = projected_pieces(core, hidden, w_qkv, devices, rows_sent)
    halves, lengths = lax.optimization_barrier((halves, lengths))
    arrived = across(halves[1], 1)
    positions = lax.optimization_barrier(lengths.astype(jnp.float32))
    cosine, sine = rotary_factors(positions)
    lengths = jnp.broadcast_to(positions[:, None], (row_count, HD))
    second = device_index % 2 == 1
    upper = device_index // (devices // 2) == 1
    signs = middle_signs(device_index, devices // 4)
    arrived, cosine, sine, lengths, other, second, upper, signs = lax.optimization_barrier(
        (arrived, cosine, sine, lengths, 1 - core, second, upper, signs)
    )
    piece = scattered_joined(halves[0], arrived).astype(jnp.bfloat16)
    mine = gathered_same_core(piece)
    theirs = across(mine, 1)
    shared = (lengths, cosine, sine, key_cache, value_cache)
    attend = lambda pair, projected: attended_pair(
        device, pair, shared[0], projected, shared[1], shared[2], shared[3], shared[4]
    )
    sent = attend(other, mine)
    arrived = across(sent, 1)
    kept = attend(core, theirs)
    if devices == H:
        parts = scattered_joined(kept, arrived)
        piece = normalized(device, parts, row_count)
        heads = gathered_at_once(piece).reshape(devices // 2, 2, row_count, HD)
        attention = heads.transpose(2, 1, 0, 3).reshape(row_count, query_width)
    else:
        held = H * row_count // devices
        first = core[0] == 0
        heads = jnp.concatenate([jnp.where(first, kept, sent), jnp.where(first, sent, kept)])
        numerators = heads[:, :row_count].reshape(devices, held, HD)
        totals = heads[:, row_count:].reshape(H // 8, 8, 8, HD)
        totals = jnp.einsum("ahhl->ahl", totals).reshape(H, HD)[:, :row_count]
        totals = jnp.pad(totals.reshape(devices, 1, held), ((0, 0), (0, 0), (0, HD - held)))
        parts = scattered_sum(jnp.concatenate([numerators, totals], axis=1), second)
        piece = (parts[:held] / parts[held, :held][:, None]).astype(jnp.bfloat16)
        heads = gathered_at_once(piece).reshape(H, row_count, HD)
        attention = heads.transpose(1, 0, 2).reshape(row_count, query_width)
    residual = (hidden_wide + jnp.dot(attention, w_out, preferred_element_type=jnp.float32)).astype(
        jnp.bfloat16
    )
    residual_full = gathered(residual, second).transpose(1, 0, 2).reshape(row_count, D)
    residual_wide = residual_full.astype(jnp.float32)
    normed = (
        residual_wide
        * lax.rsqrt(jnp.mean(residual_wide * residual_wide, axis=1, keepdims=True) + EPSILON)
    ).astype(jnp.bfloat16)
    gate = jnp.dot(normed, w_gate, preferred_element_type=jnp.float32)
    upward = jnp.dot(normed, w_up, preferred_element_type=jnp.float32)
    activation = jax.nn.silu(gate) * upward
    local_width = activation.shape[1]
    local_table = jnp.asarray(
        np.kron(sylvester_table(local_width // 28), paley_table()), dtype=jnp.float32
    )
    mixed = jnp.dot(activation, local_table, precision=lax.Precision.HIGH)
    rotated = signed_sum(mixed, second, upper, signs)
    rotated = (rotated * FF ** (-0.5)).astype(jnp.bfloat16)
    halves = down_pieces(core, rotated, w_down, devices)
    down_share = scattered_halves(halves[0], halves[1])
    return (residual.astype(jnp.float32) + down_share).astype(jnp.bfloat16)


def solution(mesh):
    in_specs = (
        P("groups", "tensor"),
        P("tensor", None),
        P("groups", "tensor", None),
        P("groups", "tensor", None),
        P("groups"),
        P(None, "tensor"),
        P(None, "tensor"),
        P(None, "tensor"),
        P("tensor", None),
    )
    out_specs = P("groups", "tensor")
    return jax.shard_map(
        per_device, mesh=mesh, in_specs=in_specs, out_specs=out_specs, check_vma=False
    )
```

```python
import jax
import jax.numpy as jnp
import numpy as np
from jax import lax
from jax.experimental import pallas as pl
from jax.experimental.pallas import tpu as pltpu
from jax.sharding import PartitionSpec as P

D = 8192
FF = 14336
H = 32
KVH = 4
HD = 128


EPSILON = 1e-05
ROPE_BASE = 500000.0
QKV_CHUNK = 2560
ROW_CHUNK = 8


def across(value, apart):
    pairs = [(source, source ^ apart) for source in range(lax.axis_size("tensor"))]
    return lax.ppermute(value, "tensor", pairs)


def same_core():
    devices = lax.axis_size("tensor")
    return [list(range(core, devices, 2)) for core in range(2)]


def scattered_sum(pieces, second):
    halves = pieces.reshape(-1, 2, *pieces.shape[1:])
    kept = jnp.where(second, halves[:, 1], halves[:, 0])
    sent = jnp.where(second, halves[:, 0], halves[:, 1]).astype(jnp.bfloat16)
    return scattered_halves(kept, sent)


def scattered_halves(kept, sent):
    return scattered_joined(kept, across(sent, 1))


def sum_kernel(parts_ref, out_ref):
    total = parts_ref[0].astype(jnp.float32)
    for index in range(1, parts_ref.shape[0]):
        total = total + parts_ref[index].astype(jnp.float32)
    out_ref[...] = total.astype(out_ref.dtype)


def summed(parts):
    vmem = pl.BlockSpec(memory_space=pltpu.VMEM)
    return pl.pallas_call(
        sum_kernel,
        out_shape=jax.ShapeDtypeStruct(parts.shape[1:], parts.dtype),
        in_specs=[vmem],
        out_specs=vmem,
        compiler_params=pltpu.CompilerParams(vmem_limit_bytes=2**20),
        cost_estimate=pl.CostEstimate(flops=4000000000, bytes_accessed=16000000, transcendentals=0),
    )(parts)


def scattered_joined(kept, arrived, short=False):
    joined = kept.astype(jnp.float32) + arrived.astype(jnp.float32)
    received = lax.all_to_all(
        joined.astype(jnp.bfloat16), "tensor", 0, 0, tiled=True, axis_index_groups=same_core()
    )
    if short:
        return summed(received)
    return jnp.sum(received.astype(jnp.float32), axis=0)


def gathered_at_once(piece):
    copies = jnp.broadcast_to(piece[None], (lax.axis_size("tensor"), *piece.shape))
    return lax.all_to_all(copies, "tensor", 0, 0, tiled=True)


def gathered_same_core(piece):
    copies = jnp.broadcast_to(piece[None], (lax.axis_size("tensor") // 2, *piece.shape))
    return lax.all_to_all(copies, "tensor", 0, 0, tiled=True, axis_index_groups=same_core())


def gathered(piece, second):
    mine = gathered_same_core(piece)
    theirs = across(mine, 1)
    both = jnp.stack([jnp.where(second, theirs, mine), jnp.where(second, mine, theirs)], axis=1)
    return both.reshape(-1, *piece.shape)


def signed_join(value, partner, upper):
    own, partner = value.astype(jnp.float32), partner.astype(jnp.float32)
    return jnp.where(upper, partner - own, own + partner)


def middle_signs(index, middle):
    common = jnp.arange(middle) & (index // 2 % middle)
    for shift in (4, 2, 1):
        common = common ^ (common >> shift)
    return 1.0 - 2.0 * (common & 1).astype(jnp.float32)


def signed_sum(value, second, upper, signs):
    devices = lax.axis_size("tensor")
    middle = devices // 4
    groups = [
        [top * devices // 2 + 2 * inner + core for inner in range(middle)]
        for top in range(2)
        for core in range(2)
    ]
    value = signed_join(value, across(value, 1), second)
    value = value.astype(jnp.bfloat16)
    value = signed_join(value, across(value, devices // 2), upper).astype(jnp.bfloat16)
    copies = jnp.broadcast_to(value[None], (middle, *value.shape))
    received = lax.all_to_all(copies, "tensor", 0, 0, tiled=True, axis_index_groups=groups)
    return jnp.sum(received.astype(jnp.float32) * signs[:, None, None], axis=0)


def normalize_kernel(device_ref, parts_ref, out_ref):
    rows = out_ref.shape[0]
    shape = (8, HD)
    chosen = lax.broadcasted_iota(jnp.int32, shape, 0) == device_ref[0] // 2 % 8
    totals = jnp.sum(jnp.where(chosen, parts_ref[rows : rows + 8], 0.0), axis=0, keepdims=True)
    shape = (rows, HD)
    own = lax.broadcasted_iota(jnp.int32, shape, 0) == lax.broadcasted_iota(jnp.int32, shape, 1)
    column = jnp.sum(jnp.where(own, totals, 0.0), axis=1, keepdims=True)
    out_ref[...] = (parts_ref[:rows] / column).astype(jnp.bfloat16)


def normalized(device, parts, rows):
    vmem = pl.BlockSpec(memory_space=pltpu.VMEM)
    return pl.pallas_call(
        normalize_kernel,
        out_shape=jax.ShapeDtypeStruct((rows, HD), jnp.bfloat16),
        in_specs=[pl.BlockSpec(memory_space=pltpu.SMEM), vmem],
        out_specs=vmem,
        compiler_params=pltpu.CompilerParams(vmem_limit_bytes=2**20),
        cost_estimate=pl.CostEstimate(flops=10000, bytes_accessed=10000, transcendentals=0),
    )(device, parts)


def in_hbm(value):
    return pltpu.with_memory_space_constraint(value, pltpu.HBM)


def column_copies(weights_ref, held_ref, arrived, chunk):
    copies = []
    for start in range(0, weights_ref.shape[1], chunk):
        part = (slice(None), pl.ds(start, chunk))
        copies.append(
            pltpu.make_async_copy(
                weights_ref.at[part], held_ref.at[part], arrived.at[start // chunk]
            )
        )
        copies[-1].start()
    return copies


def project_kernel(
    core_ref, hidden_source, source_ref, out_ref, hidden_ref, hidden_arrived, weights_ref, arrived, stacked
):
    hidden_copy = pltpu.make_async_copy(hidden_source, hidden_ref, hidden_arrived)
    hidden_copy.start()
    copies = column_copies(source_ref, weights_ref, arrived, QKV_CHUNK)
    core = core_ref[0]
    rows = hidden_ref.shape[0]
    columns = weights_ref.shape[1]
    hidden_copy.wait()
    hidden = hidden_ref[...]
    wide = hidden.astype(jnp.float32)
    squares = jnp.sum(wide * wide, axis=1, keepdims=True)
    half = stacked.shape[0] // 2
    heads = H // 2
    fresh = KVH // 2

    def place(block):
        if block < H:
            return block // heads * half + block % heads * rows
        block -= H
        kind, head = block // KVH, block % KVH
        return head // fresh * half + (heads + kind * fresh + head % fresh) * rows

    for start in range(0, columns, 2 * HD):
        if start % QKV_CHUNK == 0:
            copies[start // QKV_CHUNK].wait()
        part = jnp.dot(
            hidden, weights_ref[:, start : start + 2 * HD], preferred_element_type=jnp.float32
        )
        for offset in range(2):
            first = place(start // HD + offset)
            stacked[first : first + rows] = part[:, offset * HD : (offset + 1) * HD]
    held = out_ref.shape[2]
    for pair in range(2):
        used = pair * half + (heads + 2 * fresh) * rows
        stacked[used : used + rows] = jnp.broadcast_to(squares, (rows, HD))
        left = (pair + 1) * half - used - rows
        if left:
            stacked[used + rows : used + rows + left] = jnp.zeros((left, HD), jnp.float32)
        for piece in range(half // held):
            first = pair * half + piece * held
            values = stacked[first : first + held].astype(jnp.bfloat16)
            out_ref[pair ^ core ^ 1, piece] = values


def projected_pieces(core, hidden, w_qkv, devices, rows_sent):
    vmem = pl.BlockSpec(memory_space=pltpu.VMEM)
    return pl.pallas_call(
        project_kernel,
        out_shape=jax.ShapeDtypeStruct((2, devices // 2, rows_sent, HD), jnp.bfloat16),
        in_specs=[
            pl.BlockSpec(memory_space=pltpu.SMEM),
            pl.BlockSpec(memory_space=pltpu.HBM),
            pl.BlockSpec(memory_space=pltpu.HBM),
        ],
        out_specs=vmem,
        scratch_shapes=[
            pltpu.VMEM(hidden.shape, hidden.dtype),
            pltpu.SemaphoreType.DMA,
            pltpu.VMEM(w_qkv.shape, w_qkv.dtype),
            pltpu.SemaphoreType.DMA((w_qkv.shape[1] // QKV_CHUNK,)),
            pltpu.VMEM((devices * rows_sent, HD), jnp.float32),
        ],
        compiler_params=pltpu.CompilerParams(vmem_limit_bytes=8 * 2**20),
        cost_estimate=pl.CostEstimate(
            flops=2 * hidden.shape[0] * w_qkv.size, bytes_accessed=2 * w_qkv.size, transcendentals=0
        ),
    )(core, in_hbm(hidden), in_hbm(w_qkv))


def attend_kernel(
    device_ref, pair_ref, lengths_ref, projected_ref, cosine_ref, sine_ref, keys_ref, values_ref,
    out_ref, queries, fresh, sums,
):
    rows, slots = keys_ref.shape[:2]
    columns = pl.ds(pl.multiple_of(pair_ref[0] * 2 * HD, 2 * HD), 2 * HD)
    device = device_ref[0]
    group = H // KVH
    heads = 2 * group
    scale = HD ** (-0.5)
    cosine, sine = cosine_ref[...], sine_ref[...]
    inverse = lax.rsqrt(projected_ref[heads + 4].astype(jnp.float32) / D + EPSILON)

    def block(index):
        value = projected_ref[index].astype(jnp.float32) * inverse
        return value.astype(jnp.bfloat16).astype(jnp.float32)

    def turned(index):
        value = block(index)
        value = value * cosine + pltpu.roll(value, HD // 2, 1) * sine
        return value.astype(jnp.bfloat16).astype(jnp.float32)

    for head in range(heads):
        queries[pl.ds(head, rows, stride=heads), :] = turned(head)
    for head in range(2):
        fresh[pl.ds(head, rows, stride=4), :] = turned(heads + head)
        fresh[pl.ds(2 + head, rows, stride=4), :] = block(heads + 2 + head)

    lane = lax.broadcasted_iota(jnp.int32, (1, slots), 1) + device * slots
    lane = lane.astype(jnp.float32)
    row_lane = lax.broadcasted_iota(jnp.int32, (heads, HD), 1)
    lower = lax.broadcasted_iota(jnp.int32, (heads, HD), 0) < group

    def expand(first):
        picked = [jnp.broadcast_to(fresh[pl.ds(first + head, 1), :], (group, HD)) for head in range(2)]
        return jnp.concatenate(picked, axis=0)

    def some_rows(step, totals):
        numbers = [step * ROW_CHUNK + offset for offset in range(ROW_CHUNK)]
        scores = []
        own = []
        for row in numbers:
            query = queries[pl.ds(pl.multiple_of(row * heads, heads), heads), :]
            own_score = jnp.sum(query * expand(row * 4), axis=1, keepdims=True) * scale
            own.append(jnp.where(device == 0, jnp.exp(own_score), 0.0))
            spread = jnp.concatenate(
                [jnp.where(lower, query, 0.0), jnp.where(lower, 0.0, query)], axis=1
            ).astype(jnp.bfloat16)
            scores.append(
                lax.dot_general(
                    spread,
                    keys_ref[row, :, columns],
                    (((1,), (1,)), ((), ())),
                    preferred_element_type=jnp.float32,
                )
            )
        weights = [
            jnp.where(lane < lengths_ref[pl.ds(row, 1), :1], jnp.exp(score * scale), 0.0)
            for row, score in zip(numbers, scores)
        ]
        for row, weight, own_weight in zip(numbers, weights, own):
            product = jnp.dot(
                weight.astype(jnp.bfloat16), values_ref[row, :, columns], preferred_element_type=jnp.float32
            )
            chosen = jnp.concatenate([product[:group, :HD], product[group:, HD:]], axis=0)
            total = jnp.sum(weight, axis=1, keepdims=True) + own_weight
            summed = chosen + own_weight * expand(row * 4 + 2)
            sums[pl.ds(pl.multiple_of(row * heads, heads), heads), :] = summed
            totals = jnp.where(row_lane == row, total, totals)
        return totals

    totals = lax.fori_loop(
        0, rows // ROW_CHUNK, some_rows, jnp.zeros((heads, HD), jnp.float32)
    )
    for head in range(heads):
        start = head // 8 * 8
        values = jnp.concatenate(
            [sums[pl.ds(head, rows, stride=heads), :], totals[start : start + 8]], axis=0
        )
        out_ref[head] = values.astype(jnp.bfloat16)


def attended_pair(device, pair, lengths, projected, cosine, sine, key_cache, value_cache):
    rows, slots = key_cache.shape[0], key_cache.shape[1]
    smem = pl.BlockSpec(memory_space=pltpu.SMEM)
    vmem = pl.BlockSpec(memory_space=pltpu.VMEM)
    projected = projected.reshape(-1, HD)[: (H // 2 + 5) * rows].reshape(H // 2 + 5, rows, HD)
    return pl.pallas_call(
        attend_kernel,
        out_shape=jax.ShapeDtypeStruct((H // 2, rows + 8, HD), jnp.bfloat16),
        in_specs=[smem] * 2 + [vmem] * 6,
        out_specs=vmem,
        scratch_shapes=[
            pltpu.VMEM((rows * H // 2, HD), jnp.float32),
            pltpu.VMEM((rows * 4, HD), jnp.float32),
            pltpu.VMEM((rows * H // 2, HD), jnp.float32),
        ],
        compiler_params=pltpu.CompilerParams(vmem_limit_bytes=20 * 2**20),
        cost_estimate=pl.CostEstimate(
            flops=2 * rows * H * slots * HD,
            bytes_accessed=key_cache.size + value_cache.size,
            transcendentals=rows * H * slots // 2,
        ),
    )(device, pair, lengths, projected, cosine, sine, key_cache, value_cache)


def down_kernel(part_ref, rotated_ref, weights_ref, out_ref):
    part = part_ref[0]
    rotated = rotated_ref[...]
    pieces, _, width = out_ref.shape
    for piece in range(pieces):
        first = pl.multiple_of((2 * piece + part) * width, width)
        out_ref[piece] = jnp.dot(
            rotated, weights_ref[:, pl.ds(first, width)], preferred_element_type=jnp.float32
        ).astype(jnp.bfloat16)


def down_pieces(part, rotated, w_down, devices):
    rows = rotated.shape[0]
    width = w_down.shape[1] // devices
    vmem = pl.BlockSpec(memory_space=pltpu.VMEM)
    return pl.pallas_call(
        down_kernel,
        out_shape=jax.ShapeDtypeStruct((devices // 2, rows, width), jnp.bfloat16),
        in_specs=[pl.BlockSpec(memory_space=pltpu.SMEM), vmem, vmem],
        out_specs=vmem,
        compiler_params=pltpu.CompilerParams(vmem_limit_bytes=12 * 2**20),
        cost_estimate=pl.CostEstimate(
            flops=rows * w_down.size, bytes_accessed=w_down.size, transcendentals=0
        ),
    )(part, rotated, w_down)


def paley_table():
    prime = 13
    residues = [value * value % prime for value in range(1, prime)]
    conference = np.zeros((prime + 1, prime + 1))
    conference[0, 1:] = 1.0
    conference[1:, 0] = 1.0
    for row_number in range(prime):
        for col_number in range(prime):
            offset = (col_number - row_number) % prime
            if offset != 0:
                conference[row_number + 1, col_number + 1] = 1.0 if offset in residues else -1.0
    first_block = np.array([[1.0, -1.0], [-1.0, -1.0]])
    second_block = np.array([[1.0, 1.0], [1.0, -1.0]])
    return np.kron(conference, first_block) + np.kron(np.eye(prime + 1), second_block)


def sylvester_table(order):
    result = np.ones((1, 1))
    while result.shape[0] < order:
        result = np.kron(np.array([[1.0, 1.0], [1.0, -1.0]]), result)
    return result


def rotary_factors(positions):
    frequency = ROPE_BASE ** (-2.0 * jnp.arange(HD // 2, dtype=jnp.float32) / HD)
    angles = positions[:, None] * frequency[None, :]
    cosine, sine = jnp.cos(angles), jnp.sin(angles)
    return jnp.concatenate([cosine, cosine], axis=1), jnp.concatenate([-sine, sine], axis=1)


def per_device(hidden, w_qkv, key_cache, value_cache, lengths, w_out, w_gate, w_up, w_down):
    row_count = hidden.shape[0]
    devices = lax.axis_size("tensor")
    device_index = lax.axis_index("tensor")
    query_width = H * HD
    device = device_index.astype(jnp.int32).reshape(1)
    core = device % 2
    hidden_wide = hidden.astype(jnp.float32)
    rows_used = (H // 2 + KVH + 1) * row_count
    rows_sent = -(-rows_used // (4 * devices)) * 8
    halves = projected_pieces(core, hidden, w_qkv, devices, rows_sent)
    halves, lengths = lax.optimization_barrier((halves, lengths))
    arrived = across(halves[1], 1)
    positions = lax.optimization_barrier(lengths.astype(jnp.float32))
    cosine, sine = rotary_factors(positions)
    lengths = jnp.broadcast_to(positions[:, None], (row_count, HD))
    second = device_index % 2 == 1
    upper = device_index // (devices // 2) == 1
    signs = middle_signs(device_index, devices // 4)
    arrived, cosine, sine, lengths, other, second, upper, signs = lax.optimization_barrier(
        (arrived, cosine, sine, lengths, 1 - core, second, upper, signs)
    )
    piece = scattered_joined(halves[0], arrived, True)
    mine = gathered_same_core(piece)
    theirs = across(mine, 1)
    shared = (lengths, cosine, sine, key_cache, value_cache)
    attend = lambda pair, projected: attended_pair(
        device, pair, shared[0], projected, shared[1], shared[2], shared[3], shared[4]
    )
    sent = attend(other, mine)
    arrived = across(sent, 1)
    kept = attend(core, theirs)
    if devices == H:
        parts = scattered_joined(kept, arrived)
        piece = normalized(device, parts, row_count)
        heads = gathered_at_once(piece).reshape(devices // 2, 2, row_count, HD)
        attention = heads.transpose(2, 1, 0, 3).reshape(row_count, query_width)
    else:
        held = H * row_count // devices
        first = core[0] == 0
        heads = jnp.concatenate([jnp.where(first, kept, sent), jnp.where(first, sent, kept)])
        numerators = heads[:, :row_count].reshape(devices, held, HD)
        totals = heads[:, row_count:].reshape(H // 8, 8, 8, HD)
        totals = jnp.einsum("ahhl->ahl", totals).reshape(H, HD)[:, :row_count]
        totals = jnp.pad(totals.reshape(devices, 1, held), ((0, 0), (0, 0), (0, HD - held)))
        parts = scattered_sum(jnp.concatenate([numerators, totals], axis=1), second)
        piece = (parts[:held] / parts[held, :held][:, None]).astype(jnp.bfloat16)
        heads = gathered_at_once(piece).reshape(H, row_count, HD)
        attention = heads.transpose(1, 0, 2).reshape(row_count, query_width)
    residual = (hidden_wide + jnp.dot(attention, w_out, preferred_element_type=jnp.float32)).astype(
        jnp.bfloat16
    )
    residual_full = gathered(residual, second).transpose(1, 0, 2).reshape(row_count, D)
    residual_wide = residual_full.astype(jnp.float32)
    normed = (
        residual_wide
        * lax.rsqrt(jnp.mean(residual_wide * residual_wide, axis=1, keepdims=True) + EPSILON)
    ).astype(jnp.bfloat16)
    gate = jnp.dot(normed, w_gate, preferred_element_type=jnp.float32)
    upward = jnp.dot(normed, w_up, preferred_element_type=jnp.float32)
    activation = jax.nn.silu(gate) * upward
    local_width = activation.shape[1]
    local_table = jnp.asarray(
        np.kron(sylvester_table(local_width // 28), paley_table()), dtype=jnp.float32
    )
    mixed = jnp.dot(activation, local_table, precision=lax.Precision.HIGH)
    rotated = signed_sum(mixed, second, upper, signs)
    rotated = (rotated * FF ** (-0.5)).astype(jnp.bfloat16)
    if D // devices % HD == 0:
        sent = down_pieces(other, rotated, w_down, devices)
        arrived = across(sent, 1)
        down_share = scattered_joined(down_pieces(core, rotated, w_down, devices), arrived)
    else:
        down = jnp.dot(rotated, w_down, preferred_element_type=jnp.float32)
        down_share = scattered_sum(down.reshape(row_count, devices, -1).transpose(1, 0, 2), second)
    return (residual.astype(jnp.float32) + down_share).astype(jnp.bfloat16)


def solution(mesh):
    in_specs = (
        P("groups", "tensor"),
        P("tensor", None),
        P("groups", "tensor", None),
        P("groups", "tensor", None),
        P("groups"),
        P(None, "tensor"),
        P(None, "tensor"),
        P(None, "tensor"),
        P("tensor", None),
    )
    out_specs = P("groups", "tensor")
    return jax.shard_map(
        per_device, mesh=mesh, in_specs=in_specs, out_specs=out_specs, check_vma=False
    )
```

```python
import jax
import jax.numpy as jnp
import numpy as np
from jax import lax
from jax.experimental import pallas as pl
from jax.experimental.pallas import tpu as pltpu
from jax.sharding import PartitionSpec as P

D = 8192
FF = 14336
H = 32
KVH = 4
HD = 128


EPSILON = 1e-05
ROPE_BASE = 500000.0
QKV_CHUNK = 2560
ROW_CHUNK = 24


def across(value, apart):
    pairs = [(source, source ^ apart) for source in range(lax.axis_size("tensor"))]
    return lax.ppermute(value, "tensor", pairs)


def same_core():
    devices = lax.axis_size("tensor")
    return [list(range(core, devices, 2)) for core in range(2)]


def scattered_sum(pieces, second):
    halves = pieces.reshape(-1, 2, *pieces.shape[1:])
    kept = jnp.where(second, halves[:, 1], halves[:, 0])
    sent = jnp.where(second, halves[:, 0], halves[:, 1]).astype(jnp.bfloat16)
    return scattered_halves(kept, sent)


def scattered_halves(kept, sent):
    return scattered_joined(kept, across(sent, 1))


def sum_kernel(parts_ref, out_ref):
    total = parts_ref[0].astype(jnp.float32)
    for index in range(1, parts_ref.shape[0]):
        total = total + parts_ref[index].astype(jnp.float32)
    out_ref[...] = total.astype(out_ref.dtype)


def summed(parts):
    vmem = pl.BlockSpec(memory_space=pltpu.VMEM)
    return pl.pallas_call(
        sum_kernel,
        out_shape=jax.ShapeDtypeStruct(parts.shape[1:], parts.dtype),
        in_specs=[vmem],
        out_specs=vmem,
        compiler_params=pltpu.CompilerParams(vmem_limit_bytes=2**20),
        cost_estimate=pl.CostEstimate(flops=4000000000, bytes_accessed=16000000, transcendentals=0),
    )(parts)


def scattered_joined(kept, arrived, short=False):
    joined = kept.astype(jnp.float32) + arrived.astype(jnp.float32)
    received = lax.all_to_all(
        joined.astype(jnp.bfloat16), "tensor", 0, 0, tiled=True, axis_index_groups=same_core()
    )
    if short:
        return summed(received)
    return jnp.sum(received.astype(jnp.float32), axis=0)


def gathered_at_once(piece):
    copies = jnp.broadcast_to(piece[None], (lax.axis_size("tensor"), *piece.shape))
    return lax.all_to_all(copies, "tensor", 0, 0, tiled=True)


def gathered_same_core(piece):
    copies = jnp.broadcast_to(piece[None], (lax.axis_size("tensor") // 2, *piece.shape))
    return lax.all_to_all(copies, "tensor", 0, 0, tiled=True, axis_index_groups=same_core())


def gathered(piece, second):
    mine = gathered_same_core(piece)
    theirs = across(mine, 1)
    both = jnp.stack([jnp.where(second, theirs, mine), jnp.where(second, mine, theirs)], axis=1)
    return both.reshape(-1, *piece.shape)


def signed_join(value, partner, upper):
    own, partner = value.astype(jnp.float32), partner.astype(jnp.float32)
    return jnp.where(upper, partner - own, own + partner)


def middle_signs(index, middle):
    common = jnp.arange(middle) & (index // 2 % middle)
    for shift in (4, 2, 1):
        common = common ^ (common >> shift)
    return 1.0 - 2.0 * (common & 1).astype(jnp.float32)


def signed_sum(value, second, upper, signs):
    devices = lax.axis_size("tensor")
    middle = devices // 4
    groups = [
        [top * devices // 2 + 2 * inner + core for inner in range(middle)]
        for top in range(2)
        for core in range(2)
    ]
    value = signed_join(value, across(value, 1), second)
    value = value.astype(jnp.bfloat16)
    value = signed_join(value, across(value, devices // 2), upper).astype(jnp.bfloat16)
    copies = jnp.broadcast_to(value[None], (middle, *value.shape))
    received = lax.all_to_all(copies, "tensor", 0, 0, tiled=True, axis_index_groups=groups)
    return jnp.sum(received.astype(jnp.float32) * signs[:, None, None], axis=0)


def normalize_kernel(device_ref, parts_ref, out_ref):
    rows = out_ref.shape[0]
    shape = (8, HD)
    chosen = lax.broadcasted_iota(jnp.int32, shape, 0) == device_ref[0] // 2 % 8
    totals = jnp.sum(jnp.where(chosen, parts_ref[rows : rows + 8], 0.0), axis=0, keepdims=True)
    shape = (rows, HD)
    own = lax.broadcasted_iota(jnp.int32, shape, 0) == lax.broadcasted_iota(jnp.int32, shape, 1)
    column = jnp.sum(jnp.where(own, totals, 0.0), axis=1, keepdims=True)
    out_ref[...] = (parts_ref[:rows] / column).astype(jnp.bfloat16)


def normalized(device, parts, rows):
    vmem = pl.BlockSpec(memory_space=pltpu.VMEM)
    return pl.pallas_call(
        normalize_kernel,
        out_shape=jax.ShapeDtypeStruct((rows, HD), jnp.bfloat16),
        in_specs=[pl.BlockSpec(memory_space=pltpu.SMEM), vmem],
        out_specs=vmem,
        compiler_params=pltpu.CompilerParams(vmem_limit_bytes=2**20),
        cost_estimate=pl.CostEstimate(flops=10000, bytes_accessed=10000, transcendentals=0),
    )(device, parts)


def in_hbm(value):
    return pltpu.with_memory_space_constraint(value, pltpu.HBM)


def column_copies(weights_ref, held_ref, arrived, chunk):
    copies = []
    for start in range(0, weights_ref.shape[1], chunk):
        part = (slice(None), pl.ds(start, chunk))
        copies.append(
            pltpu.make_async_copy(
                weights_ref.at[part], held_ref.at[part], arrived.at[start // chunk]
            )
        )
        copies[-1].start()
    return copies


def project_kernel(
    core_ref, hidden_source, source_ref, out_ref, hidden_ref, hidden_arrived, weights_ref, arrived, stacked
):
    hidden_copy = pltpu.make_async_copy(hidden_source, hidden_ref, hidden_arrived)
    hidden_copy.start()
    copies = column_copies(source_ref, weights_ref, arrived, QKV_CHUNK)
    core = core_ref[0]
    rows = hidden_ref.shape[0]
    columns = weights_ref.shape[1]
    hidden_copy.wait()
    hidden = hidden_ref[...]
    wide = hidden.astype(jnp.float32)
    squares = jnp.sum(wide * wide, axis=1, keepdims=True)
    half = stacked.shape[0] // 2
    heads = H // 2
    fresh = KVH // 2

    def place(block):
        if block < H:
            return block // heads * half + block % heads * rows
        block -= H
        kind, head = block // KVH, block % KVH
        return head // fresh * half + (heads + kind * fresh + head % fresh) * rows

    for start in range(0, columns, 2 * HD):
        if start % QKV_CHUNK == 0:
            copies[start // QKV_CHUNK].wait()
        part = jnp.dot(
            hidden, weights_ref[:, start : start + 2 * HD], preferred_element_type=jnp.float32
        )
        for offset in range(2):
            first = place(start // HD + offset)
            stacked[first : first + rows] = part[:, offset * HD : (offset + 1) * HD]
    held = out_ref.shape[2]
    for pair in range(2):
        used = pair * half + (heads + 2 * fresh) * rows
        stacked[used : used + rows] = jnp.broadcast_to(squares, (rows, HD))
        left = (pair + 1) * half - used - rows
        if left:
            stacked[used + rows : used + rows + left] = jnp.zeros((left, HD), jnp.float32)
        for piece in range(half // held):
            first = pair * half + piece * held
            values = stacked[first : first + held].astype(jnp.bfloat16)
            out_ref[pair ^ core ^ 1, piece] = values


def projected_pieces(core, hidden, w_qkv, devices, rows_sent):
    vmem = pl.BlockSpec(memory_space=pltpu.VMEM)
    return pl.pallas_call(
        project_kernel,
        out_shape=jax.ShapeDtypeStruct((2, devices // 2, rows_sent, HD), jnp.bfloat16),
        in_specs=[
            pl.BlockSpec(memory_space=pltpu.SMEM),
            pl.BlockSpec(memory_space=pltpu.HBM),
            pl.BlockSpec(memory_space=pltpu.HBM),
        ],
        out_specs=vmem,
        scratch_shapes=[
            pltpu.VMEM(hidden.shape, hidden.dtype),
            pltpu.SemaphoreType.DMA,
            pltpu.VMEM(w_qkv.shape, w_qkv.dtype),
            pltpu.SemaphoreType.DMA((w_qkv.shape[1] // QKV_CHUNK,)),
            pltpu.VMEM((devices * rows_sent, HD), jnp.float32),
        ],
        compiler_params=pltpu.CompilerParams(vmem_limit_bytes=8 * 2**20),
        cost_estimate=pl.CostEstimate(
            flops=2 * hidden.shape[0] * w_qkv.size, bytes_accessed=2 * w_qkv.size, transcendentals=0
        ),
    )(core, in_hbm(hidden), in_hbm(w_qkv))


def attend_kernel(
    device_ref, pair_ref, lengths_ref, projected_ref, cosine_ref, sine_ref, keys_ref, values_ref,
    out_ref, queries, fresh, sums,
):
    rows, slots = keys_ref.shape[:2]
    columns = pl.ds(pl.multiple_of(pair_ref[0] * 2 * HD, 2 * HD), 2 * HD)
    device = device_ref[0]
    group = H // KVH
    heads = 2 * group
    scale = HD ** (-0.5)
    cosine, sine = cosine_ref[...], sine_ref[...]
    inverse = lax.rsqrt(projected_ref[heads + 4].astype(jnp.float32) / D + EPSILON)

    def block(index):
        value = projected_ref[index].astype(jnp.float32) * inverse
        return value.astype(jnp.bfloat16).astype(jnp.float32)

    def turned(index):
        value = block(index)
        value = value * cosine + pltpu.roll(value, HD // 2, 1) * sine
        return value.astype(jnp.bfloat16).astype(jnp.float32)

    for head in range(heads):
        queries[pl.ds(head, rows, stride=heads), :] = turned(head)
    for head in range(2):
        fresh[pl.ds(head, rows, stride=4), :] = turned(heads + head)
        fresh[pl.ds(2 + head, rows, stride=4), :] = block(heads + 2 + head)

    lane = lax.broadcasted_iota(jnp.int32, (1, slots), 1) + device * slots
    lane = lane.astype(jnp.float32)
    row_lane = lax.broadcasted_iota(jnp.int32, (heads, HD), 1)
    lower = lax.broadcasted_iota(jnp.int32, (heads, HD), 0) < group

    def expand(first):
        picked = [jnp.broadcast_to(fresh[pl.ds(first + head, 1), :], (group, HD)) for head in range(2)]
        return jnp.concatenate(picked, axis=0)

    def some_rows(step, totals):
        numbers = [step * ROW_CHUNK + offset for offset in range(ROW_CHUNK)]
        scores = []
        own = []
        for row in numbers:
            query = queries[pl.ds(pl.multiple_of(row * heads, heads), heads), :]
            own_score = jnp.sum(query * expand(row * 4), axis=1, keepdims=True) * scale
            own.append(jnp.where(device == 0, jnp.exp(own_score), 0.0))
            spread = jnp.concatenate(
                [jnp.where(lower, query, 0.0), jnp.where(lower, 0.0, query)], axis=1
            ).astype(jnp.bfloat16)
            scores.append(
                lax.dot_general(
                    spread,
                    keys_ref[row, :, columns],
                    (((1,), (1,)), ((), ())),
                    preferred_element_type=jnp.float32,
                )
            )
        weights = [
            jnp.where(lane < lengths_ref[pl.ds(row, 1), :1], jnp.exp(score * scale), 0.0)
            for row, score in zip(numbers, scores)
        ]
        for row, weight, own_weight in zip(numbers, weights, own):
            product = jnp.dot(
                weight.astype(jnp.bfloat16), values_ref[row, :, columns], preferred_element_type=jnp.float32
            )
            chosen = jnp.concatenate([product[:group, :HD], product[group:, HD:]], axis=0)
            total = jnp.sum(weight, axis=1, keepdims=True) + own_weight
            summed = chosen + own_weight * expand(row * 4 + 2)
            sums[pl.ds(pl.multiple_of(row * heads, heads), heads), :] = summed
            totals = jnp.where(row_lane == row, total, totals)
        return totals

    totals = lax.fori_loop(
        0, rows // ROW_CHUNK, some_rows, jnp.zeros((heads, HD), jnp.float32)
    )
    for head in range(heads):
        start = head // 8 * 8
        values = jnp.concatenate(
            [sums[pl.ds(head, rows, stride=heads), :], totals[start : start + 8]], axis=0
        )
        out_ref[head] = values.astype(jnp.bfloat16)


def attended_pair(device, pair, lengths, projected, cosine, sine, key_cache, value_cache):
    rows, slots = key_cache.shape[0], key_cache.shape[1]
    smem = pl.BlockSpec(memory_space=pltpu.SMEM)
    vmem = pl.BlockSpec(memory_space=pltpu.VMEM)
    projected = projected.reshape(-1, HD)[: (H // 2 + 5) * rows].reshape(H // 2 + 5, rows, HD)
    return pl.pallas_call(
        attend_kernel,
        out_shape=jax.ShapeDtypeStruct((H // 2, rows + 8, HD), jnp.bfloat16),
        in_specs=[smem] * 2 + [vmem] * 6,
        out_specs=vmem,
        scratch_shapes=[
            pltpu.VMEM((rows * H // 2, HD), jnp.float32),
            pltpu.VMEM((rows * 4, HD), jnp.float32),
            pltpu.VMEM((rows * H // 2, HD), jnp.float32),
        ],
        compiler_params=pltpu.CompilerParams(vmem_limit_bytes=20 * 2**20),
        cost_estimate=pl.CostEstimate(
            flops=2 * rows * H * slots * HD,
            bytes_accessed=key_cache.size + value_cache.size,
            transcendentals=rows * H * slots // 2,
        ),
    )(device, pair, lengths, projected, cosine, sine, key_cache, value_cache)


def down_kernel(part_ref, rotated_ref, weights_ref, out_ref):
    part = part_ref[0]
    rotated = rotated_ref[...]
    pieces, _, width = out_ref.shape
    for piece in range(pieces):
        first = pl.multiple_of((2 * piece + part) * width, width)
        out_ref[piece] = jnp.dot(
            rotated, weights_ref[:, pl.ds(first, width)], preferred_element_type=jnp.float32
        ).astype(jnp.bfloat16)


def down_pieces(part, rotated, w_down, devices):
    rows = rotated.shape[0]
    width = w_down.shape[1] // devices
    vmem = pl.BlockSpec(memory_space=pltpu.VMEM)
    return pl.pallas_call(
        down_kernel,
        out_shape=jax.ShapeDtypeStruct((devices // 2, rows, width), jnp.bfloat16),
        in_specs=[pl.BlockSpec(memory_space=pltpu.SMEM), vmem, vmem],
        out_specs=vmem,
        compiler_params=pltpu.CompilerParams(vmem_limit_bytes=12 * 2**20),
        cost_estimate=pl.CostEstimate(
            flops=rows * w_down.size, bytes_accessed=w_down.size, transcendentals=0
        ),
    )(part, rotated, w_down)


def paley_table():
    prime = 13
    residues = [value * value % prime for value in range(1, prime)]
    conference = np.zeros((prime + 1, prime + 1))
    conference[0, 1:] = 1.0
    conference[1:, 0] = 1.0
    for row_number in range(prime):
        for col_number in range(prime):
            offset = (col_number - row_number) % prime
            if offset != 0:
                conference[row_number + 1, col_number + 1] = 1.0 if offset in residues else -1.0
    first_block = np.array([[1.0, -1.0], [-1.0, -1.0]])
    second_block = np.array([[1.0, 1.0], [1.0, -1.0]])
    return np.kron(conference, first_block) + np.kron(np.eye(prime + 1), second_block)


def sylvester_table(order):
    result = np.ones((1, 1))
    while result.shape[0] < order:
        result = np.kron(np.array([[1.0, 1.0], [1.0, -1.0]]), result)
    return result


def rotary_factors(positions):
    frequency = ROPE_BASE ** (-2.0 * jnp.arange(HD // 2, dtype=jnp.float32) / HD)
    angles = positions[:, None] * frequency[None, :]
    cosine, sine = jnp.cos(angles), jnp.sin(angles)
    return jnp.concatenate([cosine, cosine], axis=1), jnp.concatenate([-sine, sine], axis=1)


def per_device(hidden, w_qkv, key_cache, value_cache, lengths, w_out, w_gate, w_up, w_down):
    row_count = hidden.shape[0]
    devices = lax.axis_size("tensor")
    device_index = lax.axis_index("tensor")
    query_width = H * HD
    device = device_index.astype(jnp.int32).reshape(1)
    core = device % 2
    hidden_wide = hidden.astype(jnp.float32)
    rows_used = (H // 2 + KVH + 1) * row_count
    rows_sent = -(-rows_used // (4 * devices)) * 8
    halves = projected_pieces(core, hidden, w_qkv, devices, rows_sent)
    halves, lengths = lax.optimization_barrier((halves, lengths))
    arrived = across(halves[1], 1)
    positions = lax.optimization_barrier(lengths.astype(jnp.float32))
    cosine, sine = rotary_factors(positions)
    lengths = jnp.broadcast_to(positions[:, None], (row_count, HD))
    second = device_index % 2 == 1
    upper = device_index // (devices // 2) == 1
    signs = middle_signs(device_index, devices // 4)
    arrived, cosine, sine, lengths, other, second, upper, signs = lax.optimization_barrier(
        (arrived, cosine, sine, lengths, 1 - core, second, upper, signs)
    )
    piece = scattered_joined(halves[0], arrived, True)
    mine = gathered_same_core(piece)
    theirs = across(mine, 1)
    shared = (lengths, cosine, sine, key_cache, value_cache)
    attend = lambda pair, projected: attended_pair(
        device, pair, shared[0], projected, shared[1], shared[2], shared[3], shared[4]
    )
    sent = attend(other, mine)
    arrived = across(sent, 1)
    kept = attend(core, theirs)
    if devices == H:
        parts = scattered_joined(kept, arrived)
        piece = normalized(device, parts, row_count)
        heads = gathered_at_once(piece).reshape(devices // 2, 2, row_count, HD)
        attention = heads.transpose(2, 1, 0, 3).reshape(row_count, query_width)
    else:
        held = H * row_count // devices
        first = core[0] == 0
        heads = jnp.concatenate([jnp.where(first, kept, sent), jnp.where(first, sent, kept)])
        numerators = heads[:, :row_count].reshape(devices, held, HD)
        totals = heads[:, row_count:].reshape(H // 8, 8, 8, HD)
        totals = jnp.einsum("ahhl->ahl", totals).reshape(H, HD)[:, :row_count]
        totals = jnp.pad(totals.reshape(devices, 1, held), ((0, 0), (0, 0), (0, HD - held)))
        parts = scattered_sum(jnp.concatenate([numerators, totals], axis=1), second)
        piece = (parts[:held] / parts[held, :held][:, None]).astype(jnp.bfloat16)
        heads = gathered_at_once(piece).reshape(H, row_count, HD)
        attention = heads.transpose(1, 0, 2).reshape(row_count, query_width)
    residual = (hidden_wide + jnp.dot(attention, w_out, preferred_element_type=jnp.float32)).astype(
        jnp.bfloat16
    )
    residual_full = gathered(residual, second).transpose(1, 0, 2).reshape(row_count, D)
    residual_wide = residual_full.astype(jnp.float32)
    normed = (
        residual_wide
        * lax.rsqrt(jnp.mean(residual_wide * residual_wide, axis=1, keepdims=True) + EPSILON)
    ).astype(jnp.bfloat16)
    gate = jnp.dot(normed, w_gate, preferred_element_type=jnp.float32)
    upward = jnp.dot(normed, w_up, preferred_element_type=jnp.float32)
    activation = jax.nn.silu(gate) * upward
    local_width = activation.shape[1]
    local_table = jnp.asarray(
        np.kron(sylvester_table(local_width // 28), paley_table()), dtype=jnp.float32
    )
    mixed = jnp.dot(activation, local_table, precision=lax.Precision.HIGH)
    rotated = signed_sum(mixed, second, upper, signs)
    rotated = (rotated * FF ** (-0.5)).astype(jnp.bfloat16)
    if D // devices % HD == 0:
        sent = down_pieces(other, rotated, w_down, devices)
        arrived = across(sent, 1)
        down_share = scattered_joined(down_pieces(core, rotated, w_down, devices), arrived)
    else:
        down = jnp.dot(rotated, w_down, preferred_element_type=jnp.float32)
        down_share = scattered_sum(down.reshape(row_count, devices, -1).transpose(1, 0, 2), second)
    return (residual.astype(jnp.float32) + down_share).astype(jnp.bfloat16)


def solution(mesh):
    in_specs = (
        P("groups", "tensor"),
        P("tensor", None),
        P("groups", "tensor", None),
        P("groups", "tensor", None),
        P("groups"),
        P(None, "tensor"),
        P(None, "tensor"),
        P(None, "tensor"),
        P("tensor", None),
    )
    out_specs = P("groups", "tensor")
    return jax.shard_map(
        per_device, mesh=mesh, in_specs=in_specs, out_specs=out_specs, check_vma=False
    )
```

```python
import jax
import jax.numpy as jnp
import numpy as np
from jax import lax
from jax.experimental import pallas as pl
from jax.experimental.pallas import tpu as pltpu
from jax.sharding import PartitionSpec as P

D = 8192
FF = 14336
H = 32
KVH = 4
HD = 128


EPSILON = 1e-05
ROPE_BASE = 500000.0
QKV_CHUNK = 2560
ROW_CHUNK = 24


def across(value, apart):
    pairs = [(source, source ^ apart) for source in range(lax.axis_size("tensor"))]
    return lax.ppermute(value, "tensor", pairs)


def same_core():
    devices = lax.axis_size("tensor")
    return [list(range(core, devices, 2)) for core in range(2)]


def scattered_sum(pieces, second):
    halves = pieces.reshape(-1, 2, *pieces.shape[1:])
    kept = jnp.where(second, halves[:, 1], halves[:, 0])
    sent = jnp.where(second, halves[:, 0], halves[:, 1]).astype(jnp.bfloat16)
    return scattered_halves(kept, sent)


def scattered_halves(kept, sent):
    return scattered_joined(kept, across(sent, 1))


def sum_kernel(parts_ref, out_ref):
    total = parts_ref[0].astype(jnp.float32)
    for index in range(1, parts_ref.shape[0]):
        total = total + parts_ref[index].astype(jnp.float32)
    out_ref[...] = total.astype(out_ref.dtype)


def summed(parts):
    vmem = pl.BlockSpec(memory_space=pltpu.VMEM)
    return pl.pallas_call(
        sum_kernel,
        out_shape=jax.ShapeDtypeStruct(parts.shape[1:], parts.dtype),
        in_specs=[vmem],
        out_specs=vmem,
        compiler_params=pltpu.CompilerParams(vmem_limit_bytes=2**20),
        cost_estimate=pl.CostEstimate(flops=4000000000, bytes_accessed=16000000, transcendentals=0),
    )(parts)


def scattered_joined(kept, arrived, short=False):
    joined = kept.astype(jnp.float32) + arrived.astype(jnp.float32)
    received = lax.all_to_all(
        joined.astype(jnp.bfloat16), "tensor", 0, 0, tiled=True, axis_index_groups=same_core()
    )
    if short:
        return summed(received)
    return jnp.sum(received.astype(jnp.float32), axis=0)


def gathered_at_once(piece):
    copies = jnp.broadcast_to(piece[None], (lax.axis_size("tensor"), *piece.shape))
    return lax.all_to_all(copies, "tensor", 0, 0, tiled=True)


def gathered_same_core(piece):
    copies = jnp.broadcast_to(piece[None], (lax.axis_size("tensor") // 2, *piece.shape))
    return lax.all_to_all(copies, "tensor", 0, 0, tiled=True, axis_index_groups=same_core())


def gathered(piece, second):
    mine = gathered_same_core(piece)
    theirs = across(mine, 1)
    both = jnp.stack([jnp.where(second, theirs, mine), jnp.where(second, mine, theirs)], axis=1)
    return both.reshape(-1, *piece.shape)


def signed_join(value, partner, upper):
    own, partner = value.astype(jnp.float32), partner.astype(jnp.float32)
    return jnp.where(upper, partner - own, own + partner)


def middle_signs(index, middle):
    common = jnp.arange(middle) & (index // 2 % middle)
    for shift in (4, 2, 1):
        common = common ^ (common >> shift)
    return 1.0 - 2.0 * (common & 1).astype(jnp.float32)


def signed_sum(value, second, upper, signs):
    devices = lax.axis_size("tensor")
    middle = devices // 4
    groups = [
        [top * devices // 2 + 2 * inner + core for inner in range(middle)]
        for top in range(2)
        for core in range(2)
    ]
    value = signed_join(value, across(value.astype(jnp.bfloat16), 1), second)
    value = value.astype(jnp.bfloat16)
    value = signed_join(value, across(value, devices // 2), upper).astype(jnp.bfloat16)
    copies = jnp.broadcast_to(value[None], (middle, *value.shape))
    received = lax.all_to_all(copies, "tensor", 0, 0, tiled=True, axis_index_groups=groups)
    return jnp.sum(received.astype(jnp.float32) * signs[:, None, None], axis=0)


def normalize_kernel(device_ref, parts_ref, out_ref):
    rows = out_ref.shape[0]
    shape = (8, HD)
    chosen = lax.broadcasted_iota(jnp.int32, shape, 0) == device_ref[0] // 2 % 8
    totals = jnp.sum(jnp.where(chosen, parts_ref[rows : rows + 8], 0.0), axis=0, keepdims=True)
    shape = (rows, HD)
    own = lax.broadcasted_iota(jnp.int32, shape, 0) == lax.broadcasted_iota(jnp.int32, shape, 1)
    column = jnp.sum(jnp.where(own, totals, 0.0), axis=1, keepdims=True)
    out_ref[...] = (parts_ref[:rows] / column).astype(jnp.bfloat16)


def normalized(device, parts, rows):
    vmem = pl.BlockSpec(memory_space=pltpu.VMEM)
    return pl.pallas_call(
        normalize_kernel,
        out_shape=jax.ShapeDtypeStruct((rows, HD), jnp.bfloat16),
        in_specs=[pl.BlockSpec(memory_space=pltpu.SMEM), vmem],
        out_specs=vmem,
        compiler_params=pltpu.CompilerParams(vmem_limit_bytes=2**20),
        cost_estimate=pl.CostEstimate(flops=10000, bytes_accessed=10000, transcendentals=0),
    )(device, parts)


def in_hbm(value):
    return pltpu.with_memory_space_constraint(value, pltpu.HBM)


def column_copies(weights_ref, held_ref, arrived, chunk):
    copies = []
    for start in range(0, weights_ref.shape[1], chunk):
        part = (slice(None), pl.ds(start, chunk))
        copies.append(
            pltpu.make_async_copy(
                weights_ref.at[part], held_ref.at[part], arrived.at[start // chunk]
            )
        )
        copies[-1].start()
    return copies


def project_kernel(
    core_ref, hidden_source, source_ref, out_ref, hidden_ref, hidden_arrived, weights_ref, arrived, stacked
):
    hidden_copy = pltpu.make_async_copy(hidden_source, hidden_ref, hidden_arrived)
    hidden_copy.start()
    copies = column_copies(source_ref, weights_ref, arrived, QKV_CHUNK)
    core = core_ref[0]
    rows = hidden_ref.shape[0]
    columns = weights_ref.shape[1]
    hidden_copy.wait()
    hidden = hidden_ref[...]
    wide = hidden.astype(jnp.float32)
    squares = jnp.sum(wide * wide, axis=1, keepdims=True)
    half = stacked.shape[0] // 2
    heads = H // 2
    fresh = KVH // 2

    def place(block):
        if block < H:
            return block // heads * half + block % heads * rows
        block -= H
        kind, head = block // KVH, block % KVH
        return head // fresh * half + (heads + kind * fresh + head % fresh) * rows

    for start in range(0, columns, 2 * HD):
        if start % QKV_CHUNK == 0:
            copies[start // QKV_CHUNK].wait()
        part = jnp.dot(
            hidden, weights_ref[:, start : start + 2 * HD], preferred_element_type=jnp.float32
        )
        for offset in range(2):
            first = place(start // HD + offset)
            stacked[first : first + rows] = part[:, offset * HD : (offset + 1) * HD]
    held = out_ref.shape[2]
    for pair in range(2):
        used = pair * half + (heads + 2 * fresh) * rows
        stacked[used : used + rows] = jnp.broadcast_to(squares, (rows, HD))
        left = (pair + 1) * half - used - rows
        if left:
            stacked[used + rows : used + rows + left] = jnp.zeros((left, HD), jnp.float32)
        for piece in range(half // held):
            first = pair * half + piece * held
            values = stacked[first : first + held].astype(jnp.bfloat16)
            out_ref[pair ^ core ^ 1, piece] = values


def projected_pieces(core, hidden, w_qkv, devices, rows_sent):
    vmem = pl.BlockSpec(memory_space=pltpu.VMEM)
    return pl.pallas_call(
        project_kernel,
        out_shape=jax.ShapeDtypeStruct((2, devices // 2, rows_sent, HD), jnp.bfloat16),
        in_specs=[
            pl.BlockSpec(memory_space=pltpu.SMEM),
            pl.BlockSpec(memory_space=pltpu.HBM),
            pl.BlockSpec(memory_space=pltpu.HBM),
        ],
        out_specs=vmem,
        scratch_shapes=[
            pltpu.VMEM(hidden.shape, hidden.dtype),
            pltpu.SemaphoreType.DMA,
            pltpu.VMEM(w_qkv.shape, w_qkv.dtype),
            pltpu.SemaphoreType.DMA((w_qkv.shape[1] // QKV_CHUNK,)),
            pltpu.VMEM((devices * rows_sent, HD), jnp.float32),
        ],
        compiler_params=pltpu.CompilerParams(vmem_limit_bytes=8 * 2**20),
        cost_estimate=pl.CostEstimate(
            flops=2 * hidden.shape[0] * w_qkv.size, bytes_accessed=2 * w_qkv.size, transcendentals=0
        ),
    )(core, in_hbm(hidden), in_hbm(w_qkv))


def attend_kernel(
    device_ref, pair_ref, lengths_ref, projected_ref, cosine_ref, sine_ref, keys_ref, values_ref,
    out_ref, queries, fresh, sums,
):
    rows, slots = keys_ref.shape[:2]
    columns = pl.ds(pl.multiple_of(pair_ref[0] * 2 * HD, 2 * HD), 2 * HD)
    device = device_ref[0]
    group = H // KVH
    heads = 2 * group
    scale = HD ** (-0.5)
    cosine, sine = cosine_ref[...], sine_ref[...]
    inverse = lax.rsqrt(projected_ref[heads + 4].astype(jnp.float32) / D + EPSILON)

    def block(index):
        value = projected_ref[index].astype(jnp.float32) * inverse
        return value.astype(jnp.bfloat16).astype(jnp.float32)

    def turned(index):
        value = block(index)
        value = value * cosine + pltpu.roll(value, HD // 2, 1) * sine
        return value.astype(jnp.bfloat16).astype(jnp.float32)

    for head in range(heads):
        queries[pl.ds(head, rows, stride=heads), :] = turned(head)
    for head in range(2):
        fresh[pl.ds(head, rows, stride=4), :] = turned(heads + head)
        fresh[pl.ds(2 + head, rows, stride=4), :] = block(heads + 2 + head)

    lane = lax.broadcasted_iota(jnp.int32, (1, slots), 1) + device * slots
    lane = lane.astype(jnp.float32)
    row_lane = lax.broadcasted_iota(jnp.int32, (heads, HD), 1)
    lower = lax.broadcasted_iota(jnp.int32, (heads, HD), 0) < group

    def expand(first):
        picked = [jnp.broadcast_to(fresh[pl.ds(first + head, 1), :], (group, HD)) for head in range(2)]
        return jnp.concatenate(picked, axis=0)

    def some_rows(step, totals):
        numbers = [step * ROW_CHUNK + offset for offset in range(ROW_CHUNK)]
        scores = []
        own = []
        for row in numbers:
            query = queries[pl.ds(pl.multiple_of(row * heads, heads), heads), :]
            own_score = jnp.sum(query * expand(row * 4), axis=1, keepdims=True) * scale
            own.append(jnp.where(device == 0, jnp.exp(own_score), 0.0))
            spread = jnp.concatenate(
                [jnp.where(lower, query, 0.0), jnp.where(lower, 0.0, query)], axis=1
            ).astype(jnp.bfloat16)
            scores.append(
                lax.dot_general(
                    spread,
                    keys_ref[row, :, columns],
                    (((1,), (1,)), ((), ())),
                    preferred_element_type=jnp.float32,
                )
            )
        weights = [
            jnp.where(lane < lengths_ref[pl.ds(row, 1), :1], jnp.exp(score * scale), 0.0)
            for row, score in zip(numbers, scores)
        ]
        for row, weight, own_weight in zip(numbers, weights, own):
            product = jnp.dot(
                weight.astype(jnp.bfloat16), values_ref[row, :, columns], preferred_element_type=jnp.float32
            )
            chosen = jnp.concatenate([product[:group, :HD], product[group:, HD:]], axis=0)
            total = jnp.sum(weight, axis=1, keepdims=True) + own_weight
            summed = chosen + own_weight * expand(row * 4 + 2)
            sums[pl.ds(pl.multiple_of(row * heads, heads), heads), :] = summed
            totals = jnp.where(row_lane == row, total, totals)
        return totals

    totals = lax.fori_loop(
        0, rows // ROW_CHUNK, some_rows, jnp.zeros((heads, HD), jnp.float32)
    )
    for head in range(heads):
        start = head // 8 * 8
        values = jnp.concatenate(
            [sums[pl.ds(head, rows, stride=heads), :], totals[start : start + 8]], axis=0
        )
        out_ref[head] = values.astype(jnp.bfloat16)


def attended_pair(device, pair, lengths, projected, cosine, sine, key_cache, value_cache):
    rows, slots = key_cache.shape[0], key_cache.shape[1]
    smem = pl.BlockSpec(memory_space=pltpu.SMEM)
    vmem = pl.BlockSpec(memory_space=pltpu.VMEM)
    projected = projected.reshape(-1, HD)[: (H // 2 + 5) * rows].reshape(H // 2 + 5, rows, HD)
    return pl.pallas_call(
        attend_kernel,
        out_shape=jax.ShapeDtypeStruct((H // 2, rows + 8, HD), jnp.bfloat16),
        in_specs=[smem] * 2 + [vmem] * 6,
        out_specs=vmem,
        scratch_shapes=[
            pltpu.VMEM((rows * H // 2, HD), jnp.float32),
            pltpu.VMEM((rows * 4, HD), jnp.float32),
            pltpu.VMEM((rows * H // 2, HD), jnp.float32),
        ],
        compiler_params=pltpu.CompilerParams(vmem_limit_bytes=20 * 2**20),
        cost_estimate=pl.CostEstimate(
            flops=2 * rows * H * slots * HD,
            bytes_accessed=key_cache.size + value_cache.size,
            transcendentals=rows * H * slots // 2,
        ),
    )(device, pair, lengths, projected, cosine, sine, key_cache, value_cache)


def down_kernel(part_ref, rotated_ref, weights_ref, out_ref):
    part = part_ref[0]
    rotated = rotated_ref[...]
    pieces, _, width = out_ref.shape
    for piece in range(pieces):
        first = pl.multiple_of((2 * piece + part) * width, width)
        out_ref[piece] = jnp.dot(
            rotated, weights_ref[:, pl.ds(first, width)], preferred_element_type=jnp.float32
        ).astype(jnp.bfloat16)


def down_pieces(part, rotated, w_down, devices):
    rows = rotated.shape[0]
    width = w_down.shape[1] // devices
    vmem = pl.BlockSpec(memory_space=pltpu.VMEM)
    return pl.pallas_call(
        down_kernel,
        out_shape=jax.ShapeDtypeStruct((devices // 2, rows, width), jnp.bfloat16),
        in_specs=[pl.BlockSpec(memory_space=pltpu.SMEM), vmem, vmem],
        out_specs=vmem,
        compiler_params=pltpu.CompilerParams(vmem_limit_bytes=12 * 2**20),
        cost_estimate=pl.CostEstimate(
            flops=rows * w_down.size, bytes_accessed=w_down.size, transcendentals=0
        ),
    )(part, rotated, w_down)


def paley_table():
    prime = 13
    residues = [value * value % prime for value in range(1, prime)]
    conference = np.zeros((prime + 1, prime + 1))
    conference[0, 1:] = 1.0
    conference[1:, 0] = 1.0
    for row_number in range(prime):
        for col_number in range(prime):
            offset = (col_number - row_number) % prime
            if offset != 0:
                conference[row_number + 1, col_number + 1] = 1.0 if offset in residues else -1.0
    first_block = np.array([[1.0, -1.0], [-1.0, -1.0]])
    second_block = np.array([[1.0, 1.0], [1.0, -1.0]])
    return np.kron(conference, first_block) + np.kron(np.eye(prime + 1), second_block)


def sylvester_table(order):
    result = np.ones((1, 1))
    while result.shape[0] < order:
        result = np.kron(np.array([[1.0, 1.0], [1.0, -1.0]]), result)
    return result


def rotary_factors(positions):
    frequency = ROPE_BASE ** (-2.0 * jnp.arange(HD // 2, dtype=jnp.float32) / HD)
    angles = positions[:, None] * frequency[None, :]
    cosine, sine = jnp.cos(angles), jnp.sin(angles)
    return jnp.concatenate([cosine, cosine], axis=1), jnp.concatenate([-sine, sine], axis=1)


def per_device(hidden, w_qkv, key_cache, value_cache, lengths, w_out, w_gate, w_up, w_down):
    row_count = hidden.shape[0]
    devices = lax.axis_size("tensor")
    device_index = lax.axis_index("tensor")
    query_width = H * HD
    device = device_index.astype(jnp.int32).reshape(1)
    core = device % 2
    hidden_wide = hidden.astype(jnp.float32)
    rows_used = (H // 2 + KVH + 1) * row_count
    rows_sent = -(-rows_used // (4 * devices)) * 8
    halves = projected_pieces(core, hidden, w_qkv, devices, rows_sent)
    halves, lengths = lax.optimization_barrier((halves, lengths))
    arrived = across(halves[1], 1)
    positions = lax.optimization_barrier(lengths.astype(jnp.float32))
    cosine, sine = rotary_factors(positions)
    lengths = jnp.broadcast_to(positions[:, None], (row_count, HD))
    second = device_index % 2 == 1
    upper = device_index // (devices // 2) == 1
    signs = middle_signs(device_index, devices // 4)
    arrived, cosine, sine, lengths, other, second, upper, signs = lax.optimization_barrier(
        (arrived, cosine, sine, lengths, 1 - core, second, upper, signs)
    )
    piece = scattered_joined(halves[0], arrived, True)
    mine = gathered_same_core(piece)
    theirs = across(mine, 1)
    shared = (lengths, cosine, sine, key_cache, value_cache)
    attend = lambda pair, projected: attended_pair(
        device, pair, shared[0], projected, shared[1], shared[2], shared[3], shared[4]
    )
    sent = attend(other, mine)
    arrived = across(sent, 1)
    kept = attend(core, theirs)
    if devices == H:
        parts = scattered_joined(kept, arrived)
        piece = normalized(device, parts, row_count)
        heads = gathered_at_once(piece).reshape(devices // 2, 2, row_count, HD)
        attention = heads.transpose(2, 1, 0, 3).reshape(row_count, query_width)
    else:
        held = H * row_count // devices
        first = core[0] == 0
        heads = jnp.concatenate([jnp.where(first, kept, sent), jnp.where(first, sent, kept)])
        numerators = heads[:, :row_count].reshape(devices, held, HD)
        totals = heads[:, row_count:].reshape(H // 8, 8, 8, HD)
        totals = jnp.einsum("ahhl->ahl", totals).reshape(H, HD)[:, :row_count]
        totals = jnp.pad(totals.reshape(devices, 1, held), ((0, 0), (0, 0), (0, HD - held)))
        parts = scattered_sum(jnp.concatenate([numerators, totals], axis=1), second)
        piece = (parts[:held] / parts[held, :held][:, None]).astype(jnp.bfloat16)
        heads = gathered_at_once(piece).reshape(H, row_count, HD)
        attention = heads.transpose(1, 0, 2).reshape(row_count, query_width)
    residual = (hidden_wide + jnp.dot(attention, w_out, preferred_element_type=jnp.float32)).astype(
        jnp.bfloat16
    )
    residual_full = gathered(residual, second).transpose(1, 0, 2).reshape(row_count, D)
    residual_wide = residual_full.astype(jnp.float32)
    normed = (
        residual_wide
        * lax.rsqrt(jnp.mean(residual_wide * residual_wide, axis=1, keepdims=True) + EPSILON)
    ).astype(jnp.bfloat16)
    gate = jnp.dot(normed, w_gate, preferred_element_type=jnp.float32)
    upward = jnp.dot(normed, w_up, preferred_element_type=jnp.float32)
    activation = jax.nn.silu(gate) * upward
    local_width = activation.shape[1]
    local_table = jnp.asarray(
        np.kron(sylvester_table(local_width // 28), paley_table()), dtype=jnp.float32
    )
    mixed = jnp.dot(activation, local_table, precision=lax.Precision.HIGH)
    rotated = signed_sum(mixed, second, upper, signs)
    rotated = (rotated * FF ** (-0.5)).astype(jnp.bfloat16)
    if D // devices % HD == 0:
        sent = down_pieces(other, rotated, w_down, devices)
        arrived = across(sent, 1)
        down_share = scattered_joined(down_pieces(core, rotated, w_down, devices), arrived)
    else:
        down = jnp.dot(rotated, w_down, preferred_element_type=jnp.float32)
        down_share = scattered_sum(down.reshape(row_count, devices, -1).transpose(1, 0, 2), second)
    return (residual.astype(jnp.float32) + down_share).astype(jnp.bfloat16)


def solution(mesh):
    in_specs = (
        P("groups", "tensor"),
        P("tensor", None),
        P("groups", "tensor", None),
        P("groups", "tensor", None),
        P("groups"),
        P(None, "tensor"),
        P(None, "tensor"),
        P(None, "tensor"),
        P("tensor", None),
    )
    out_specs = P("groups", "tensor")
    return jax.shard_map(
        per_device, mesh=mesh, in_specs=in_specs, out_specs=out_specs, check_vma=False
    )
```
